32 devices in a mesh: pipe: 2 (over core), expert: 16 (over z, y, x).
Axes of the slice: x: 2, y: 2, z: 4, core: 2. Of those that a mesh axis runs over, the one named last changes fastest.
Arguments:
- tokens: bfloat16 [4096, 7168], P(('pipe', 'expert')), may hold values from -6 to 6
- cotangent: bfloat16 [4096, 7168], P(('pipe', 'expert')), may hold values from -6 to 6
- expert_ids: int32 [4096, 8], P(('pipe', 'expert')), may hold values from 0 to 255, all different within a row; in each aligned block of 128 rows (0 to 127, 128 to 255, ...) at most 8 rows name the same one
- gate_weights: float32 [4096, 8], P(('pipe', 'expert')), may hold values from 0.1 to 0.6
- w_gate: bfloat16 [2, 3584, 2048], P('pipe', None, 'expert'), may hold values from -0.0625 to 0.0625
- w_up: bfloat16 [2, 3584, 2048], P('pipe', None, 'expert'), may hold values from -0.0625 to 0.0625
- w_down: bfloat16 [2, 2048, 3584], P('pipe', 'expert'), may hold values from -0.1875 to 0.1875
Outputs:
- mixed_out: bfloat16 [4096, 7168], P(('pipe', 'expert'))
- input_grad: bfloat16 [4096, 7168], P(('pipe', 'expert'))
- grad_gate: bfloat16 [2, 3584, 2048], P('pipe', None, 'expert')
- grad_up: bfloat16 [2, 3584, 2048], P('pipe', None, 'expert')
- grad_down: bfloat16 [2, 2048, 3584], P('pipe', 'expert')
The draws below stay inside these ranges and needn't reach their ends.
Inputs may be any that keep to these rules, and one draw needn't show every extreme that they name: `expert_ids`: the 8 entries of a row differ. In each block of 128 rows, no expert is named more than 8 times, a bound that some block reaches.
All inputs are finite; a program needn't handle non-finite values.
Results may differ from the reference program's by a relative error of at most 0.0065.
Values may be sent and summed in bfloat16 or wider, within the bound.
No kernel may reach another device: no remote copies, remote signals or barrier semaphores. Data moves between devices by JAX's collectives and lax.ppermute only.
A program may use at most 128 MiB of HBM per device.

```python
import math
import jax
import jax.numpy as jnp
import numpy as np
from jax import lax

D = 7168
HE = 1024
ROUTED = 256
TOP = 8
GROUP = 8
TOK_DEV = 128
CAP = 8
HE_DEV = 128
D2 = 3584
EXPERTS = 2
TOKENS = 4096
N_PIPE = 2
N_EXPERT = 16


def level_of(own_key, dims, split, smallest, high):
    loudness, own = 1.0, jax.random.fold_in(own_key, 6)
    for position, parts in split:
        draws = jnp.exp(jax.random.uniform(jax.random.fold_in(own, position), (parts,), jnp.float32, smallest / len(split), high / len(split)))
        loudness = loudness * jnp.repeat(draws, dims[position] // parts).reshape([-1 if axis == position else 1 for axis in range(len(dims))])
    return loudness


def assign_block(own_key, own, number, rows, count, top, most, slope):
    sequence = jax.random.permutation(own_key, count)
    heavy_load, ordinary = load_shares(count, rows * top, most, slope, True), load_shares(count, rows * top, most, slope, False)
    places = jnp.arange(count)

    def named(tallies, turn):
        used = int((tallies > 0).sum())
        fixed = max(1, used // 4)
        moved = fixed + (places - fixed + turn * (used - fixed)) % max(1, count - fixed)
        return jnp.zeros((count,), jnp.int32).at[sequence[jnp.where(places < fixed, places, moved)]].set(jnp.asarray(tallies, jnp.int32))

    tallies = jnp.where(number % 4 == 0, named(heavy_load, number // 4), named(ordinary, number - number // 4 - 1))
    mixed = jax.random.permutation(jax.random.fold_in(own, 3), count)
    source_of, sink = mixed[0:count // 2 * 2:2], mixed[1:count // 2 * 2:2]
    room = jnp.minimum(tallies[source_of] - 1, most - tallies[sink]) // 2
    room = jnp.where((source_of == sequence[0]) | (sink == sequence[0]) | (tallies[sink] == 0), 0, jnp.maximum(room, 0))
    moved = jax.random.randint(jax.random.fold_in(own, 4), (count // 2,), 0, 1 << 20) % (room + 1)
    tallies = tallies.at[source_of].add(-moved).at[sink].add(moved)
    items = jnp.searchsorted(jnp.cumsum(tallies), jnp.arange(rows * top), side="right").astype(jnp.int32)
    grid = items.reshape(top, rows).T
    grid = grid[jax.random.permutation(jax.random.fold_in(own, 1), rows)]
    turn = jax.random.randint(jax.random.fold_in(own, 2), (rows, 1), 0, top)
    return jnp.take_along_axis(grid, (jnp.arange(top)[None, :] + turn) % top, axis=1)


def load_shares(number_of, total, limit, slope, full):
    loads = [(1 << 20) // math.isqrt(rank ** slope) + 1 for rank in range(1, number_of + 1)]
    largest = limit if full else min(limit, max(-(-total // number_of), total * loads[0] // sum(loads)))
    least = 1 if total - largest >= number_of - 1 else 0
    counts, surplus = [largest] + [least] * (number_of - 1), total - largest - least * (number_of - 1)
    while surplus > 0:
        free = [i for i in range(1, number_of) if counts[i] < largest] or [i for i in range(1, number_of) if counts[i] < limit]
        whole, left = sum([loads[i] for i in free]), surplus
        for i in free:
            addition = min(limit - counts[i], max(1, left * loads[i] // whole), surplus)
            counts[i] = counts[i] + addition
            surplus = surplus - addition
    return np.array(counts)


def gaussian(stream_key, shape, spread, reach, cuts=(), kind=jnp.bfloat16):
    values = jax.random.normal(stream_key, shape, jnp.float32) * spread
    if len(cuts) > 0:
        values = level_of(stream_key, shape, cuts, -0.22, 0.18) * values
    return jnp.clip(values, min=-reach, max=reach).astype(kind)


def setup_inputs(seed: int = 0) -> dict:
    splits = jax.random.split(jax.random.key(seed), 8)
    tokens = gaussian(splits[0], (TOKENS, D), 1.0, 6.0, ((0, 32),))
    cotangent = gaussian(splits[1], (TOKENS, D), 1.0, 6.0, ((0, 32),))
    expert_ids_keys = jax.random.split(jax.random.fold_in(splits[2], 1), TOKENS // TOK_DEV)
    expert_ids_turns = jax.random.permutation(jax.random.fold_in(splits[2], 3), TOKENS // TOK_DEV)
    expert_ids = jax.vmap(lambda own, number: assign_block(jax.random.fold_in(splits[2], 2), own, number, TOK_DEV, ROUTED, TOP, CAP, 2))(expert_ids_keys, expert_ids_turns).reshape((TOKENS, TOP))
    gate_weights = jnp.clip(0.1 + 0.5 * jax.random.uniform(splits[3], (TOKENS, TOP), jnp.float32) ** level_of(splits[3], (TOKENS, TOP), ((0, 32),), -0.2, 0.2), 0.1, 0.6)
    w_gate = gaussian(splits[4], (N_PIPE, D2, EXPERTS * HE), D ** -0.5, 0.0625, ((0, 2), (2, 16)))
    w_up = gaussian(splits[5], (N_PIPE, D2, EXPERTS * HE), D ** -0.5, 0.0625, ((0, 2), (2, 16)))
    w_down = gaussian(splits[6], (N_PIPE, EXPERTS * HE, D2), HE ** -0.5, 0.1875, ((0, 2), (1, 16)))
    return {"tokens": tokens, "cotangent": cotangent, "expert_ids": expert_ids, "gate_weights": gate_weights, "w_gate": w_gate, "w_up": w_up, "w_down": w_down}


def round_trip(values):
    return lax.optimization_barrier(values.astype(jnp.bfloat16)).astype(jnp.float32)


def route_tables(expert_ids, gate_weights):
    experts = jnp.arange(EXPERTS, dtype=jnp.int32)
    match = (expert_ids[..., None] == experts).astype(jnp.float32)
    hits = jnp.sum(match, axis=-2)
    chosen = jnp.sum(match * gate_weights[..., None], axis=-2)
    slots = jnp.cumsum(hits, axis=-2) - 1.0
    levels = jnp.arange(CAP, dtype=jnp.float32)
    place = hits[..., None] * (slots[..., None] == levels).astype(jnp.float32)
    return place, chosen


def expert_pass(slot_rows, scaled, gate_cols, up_cols, down_rows):
    width = slot_rows.shape[1]
    gate_pre = jnp.dot(slot_rows, gate_cols, preferred_element_type=jnp.float32)
    up_pre = jnp.dot(slot_rows, up_cols, preferred_element_type=jnp.float32)
    sigma = jax.nn.sigmoid(gate_pre)
    active = gate_pre * sigma
    hidden = (active * up_pre).astype(jnp.bfloat16)
    hidden_parts = hidden.reshape(-1, GROUP, HE_DEV).astype(jnp.float32)
    down_parts = down_rows.reshape(GROUP, HE_DEV, width).astype(jnp.float32)
    out_parts = jnp.einsum('rmk,mkd->mrd', hidden_parts, down_parts)
    expert_out = jnp.sum(round_trip(out_parts), axis=0)
    dhidden = jnp.dot(scaled, down_rows.T, preferred_element_type=jnp.float32)
    dgate = (dhidden * up_pre * sigma * (1.0 + gate_pre * (1.0 - sigma))).astype(jnp.bfloat16)
    dup = (dhidden * active).astype(jnp.bfloat16)
    gate_parts = gate_cols.reshape(width, GROUP, HE_DEV).astype(jnp.float32)
    up_parts = up_cols.reshape(width, GROUP, HE_DEV).astype(jnp.float32)
    dx_parts = jnp.einsum('rmk,dmk->mrd', dgate.reshape(-1, GROUP, HE_DEV).astype(jnp.float32), gate_parts)
    dx_parts = dx_parts + jnp.einsum('rmk,dmk->mrd', dup.reshape(-1, GROUP, HE_DEV).astype(jnp.float32), up_parts)
    dx_rows = jnp.sum(round_trip(dx_parts), axis=0)
    grad_g = jnp.dot(slot_rows.T, dgate, preferred_element_type=jnp.float32)
    grad_u = jnp.dot(slot_rows.T, dup, preferred_element_type=jnp.float32)
    grad_d = jnp.dot(hidden.T, scaled, preferred_element_type=jnp.float32)
    return expert_out, dx_rows, grad_g, grad_u, grad_d


def rank_pass(rank_tokens, rank_cot, rank_ids, rank_gates, gate_full, up_full, down_full):
    place, chosen = route_tables(rank_ids, rank_gates)
    highest = lax.Precision.HIGHEST
    tok_f = rank_tokens.astype(jnp.float32)
    cot_f = rank_cot.astype(jnp.float32)
    rows_all = jnp.einsum('ntec,ntd->encd', place, tok_f, precision=highest).astype(jnp.bfloat16)
    gate_slot = jnp.einsum('ntec,nte->enc', place, chosen, precision=highest)
    raw_cot = jnp.einsum('ntec,ntd->encd', place, cot_f, precision=highest)
    scaled_all = (gate_slot[..., None] * raw_cot).astype(jnp.bfloat16)
    blocks = rank_tokens.shape[0]
    mixed = jnp.zeros(rank_tokens.shape, jnp.float32)
    dinput = jnp.zeros(rank_tokens.shape, jnp.float32)
    grads_g, grads_u, grads_d = [], [], []
    for expert in range(EXPERTS):
        lower = expert * HE
        result = expert_pass(rows_all[expert].reshape(blocks * CAP, D), scaled_all[expert].reshape(blocks * CAP, D),
                             gate_full[:, lower:lower + HE], up_full[:, lower:lower + HE], down_full[lower:lower + HE, :])
        expert_out, dx_rows, grad_g, grad_u, grad_d = result
        weighted = gate_slot[expert][..., None] * expert_out.reshape(blocks, CAP, D)
        mixed = mixed + jnp.einsum('ntc,ncd->ntd', place[:, :, expert, :], weighted, precision=highest)
        dinput = dinput + jnp.einsum('ntc,ncd->ntd', place[:, :, expert, :], dx_rows.reshape(blocks, CAP, D), precision=highest)
        grads_g.append(grad_g)
        grads_u.append(grad_u)
        grads_d.append(grad_d)
    return (mixed.astype(jnp.bfloat16), dinput.astype(jnp.bfloat16), jnp.concatenate(grads_g, axis=1),
            jnp.concatenate(grads_u, axis=1), jnp.concatenate(grads_d, axis=0))


def reference(tokens, cotangent, expert_ids, gate_weights, w_gate, w_up, w_down):
    half_pipe = N_PIPE // 2
    token_blocks = tokens.reshape(N_PIPE, N_EXPERT, TOK_DEV, D)
    cot_blocks = cotangent.reshape(N_PIPE, N_EXPERT, TOK_DEV, D)
    id_blocks = expert_ids.reshape(N_PIPE, N_EXPERT, TOK_DEV, TOP)
    gate_blocks = gate_weights.reshape(N_PIPE, N_EXPERT, TOK_DEV, TOP)

    def pair_pass(pair_index):
        front = pair_index
        back = N_PIPE - 1 - pair_index
        gate_full = jnp.concatenate([w_gate[front], w_gate[back]], axis=0)
        up_full = jnp.concatenate([w_up[front], w_up[back]], axis=0)
        down_full = jnp.concatenate([w_down[front], w_down[back]], axis=1)
        front_res = rank_pass(token_blocks[front], cot_blocks[front], id_blocks[front], gate_blocks[front], gate_full, up_full, down_full)
        back_res = rank_pass(token_blocks[back], cot_blocks[back], id_blocks[back], gate_blocks[back], gate_full, up_full, down_full)
        sum_g = round_trip(front_res[2]) + round_trip(back_res[2])
        sum_u = round_trip(front_res[3]) + round_trip(back_res[3])
        sum_d = round_trip(front_res[4]) + round_trip(back_res[4])
        return (front_res[0], back_res[0], front_res[1], back_res[1],
                sum_g[:D2].astype(jnp.bfloat16), sum_g[D2:].astype(jnp.bfloat16),
                sum_u[:D2].astype(jnp.bfloat16), sum_u[D2:].astype(jnp.bfloat16),
                sum_d[:, :D2].astype(jnp.bfloat16), sum_d[:, D2:].astype(jnp.bfloat16))

    mapped = lax.map(pair_pass, jnp.arange(half_pipe, dtype=jnp.int32))

    def assemble(front_stack, back_stack):
        return jnp.concatenate([front_stack, back_stack[::-1]], axis=0)

    mixed_out = assemble(mapped[0], mapped[1]).reshape(TOKENS, D)
    input_grad = assemble(mapped[2], mapped[3]).reshape(TOKENS, D)
    grad_gate = assemble(mapped[4], mapped[5])
    grad_up = assemble(mapped[6], mapped[7])
    grad_down = assemble(mapped[8], mapped[9])
    return mixed_out, input_grad, grad_gate, grad_up, grad_down
```

```python
import functools

import jax
import jax.numpy as jnp
from jax import lax
from jax.experimental import pallas as pl
from jax.experimental.pallas import tpu as pltpu
from jax.sharding import PartitionSpec as P

GROUP = 8
CAP = 8
BF16, F32 = jnp.bfloat16, jnp.float32
AXES = ("pipe", "expert")
VMEM = pl.BlockSpec(memory_space=pltpu.VMEM)
ANY = pl.BlockSpec(memory_space=pl.ANY)
LIMIT = 16 * 1024 * 1024


TREES = {
    "A": {4: (0, 2), 1: (0, 0), 2: (0, 1), 5: (1, 2), 6: (4, 1), 3: (2, 0), 7: (5, 1)},
    "B": {4: (0, 2), 2: (0, 1), 1: (0, 0), 5: (4, 0), 6: (2, 2), 3: (1, 1), 7: (3, 2)},
    "C": {4: (0, 2), 1: (0, 0), 2: (0, 1), 5: (4, 0), 6: (4, 1), 3: (1, 1), 7: (3, 2)},
    "D": {2: (0, 1), 4: (0, 2), 1: (0, 0), 5: (1, 2), 6: (4, 1), 3: (2, 0), 7: (3, 2)},
}

AFTER = {
    "D4": ["C4", "C5"],
    "B5": ["B1", "A6", "A3"],
    "A6": ["A2"],
    "C4": ["D"],
    "B4": ["A4"],
    "C3": ["D7"],
    "B1": ["A1"],
    "near_back": ["D5", "D6"],
    "far_back": ["C2"],
    "merged": ["near_back"],
    "B0": ["near_there"],
    "A3": ["A2"],
    "C1": ["C3"],
    "A7": ["A1"],
}

COST = {"near_back": 4000000, "far_back": 1000000, "select": 20000000, "merged": 4000000, "inner": 4000000}


def moved(block, mirror, step):
    ranks, owners = lax.axis_size("pipe"), lax.axis_size("expert")
    route = []
    for rank in range(ranks):
        target = ranks - 1 - rank if mirror else rank
        for index in range(owners):
            route.append((rank * owners + index, target * owners + (index + step * GROUP) % owners))
    return lax.ppermute(block, AXES, route)


def neighbour(block, bit):
    owners = lax.axis_size("expert")
    return lax.ppermute(block, "expert", [(index, index ^ 1 << bit) for index in range(owners)])


def dot(a, b, contract=(1, 0)):
    return lax.dot_general(
        a, b, (((contract[0],), (contract[1],)), ((), ())), preferred_element_type=F32
    )


def call(kernel, shapes, operands, after=(), far=(), far_out=0, scratch=(), cost=1, alias=None, limit=LIMIT):
    out = [jax.ShapeDtypeStruct(shape, dtype) for shape, dtype in shapes]
    count = len(operands)
    specs = [ANY if i in far else VMEM for i in range(count)]

    def body(*refs):
        kernel(*refs[:count], *refs[count + len(after) :])

    results = pl.pallas_call(
        body,
        out_shape=out,
        in_specs=specs + [ANY] * len(after),
        out_specs=[ANY if i < far_out else VMEM for i in range(len(out))],
        scratch_shapes=list(scratch),
        input_output_aliases=alias or {},
        compiler_params=pltpu.CompilerParams(vmem_limit_bytes=limit),
        cost_estimate=pl.CostEstimate(flops=1, bytes_accessed=cost, transcendentals=0),
    )(*operands, *after)
    return list(results)


def copy_kernel(block, out):
    out[...] = block[...]


def add_kernel(*refs):
    total = refs[0][...].astype(F32)
    for ref in refs[1:-1]:
        total = total + ref[...].astype(F32)
    refs[-1][...] = total.astype(BF16)


def join_kernel(*refs):
    for index in range(0, len(refs) - 1, 2):
        own, other = refs[index][...].astype(F32), refs[index + 1][...].astype(F32)
        unit = jnp.concatenate([own[:CAP], other[:CAP], own[CAP:], other[CAP:]], axis=0)
        refs[-1][pl.ds(index * 2 * CAP, 4 * CAP), :] = unit.astype(BF16)


def split_sum_kernel(arrived, *refs):
    blocks, pieces = refs[: arrived + 1], refs[arrived + 1 :]
    for index in range(0, len(pieces), 2):
        rows = pl.ds(index * 2 * CAP, 4 * CAP)
        unit = blocks[0][rows, :].astype(F32)
        for block in blocks[1:]:
            unit = unit + block[rows, :].astype(F32)
        parts = [unit[place * CAP : (place + 1) * CAP] for place in range(4)]
        pieces[index][...] = jnp.concatenate(parts[0::2], axis=0).astype(BF16)
        pieces[index + 1][...] = jnp.concatenate(parts[1::2], axis=0).astype(BF16)


def halves_of(middle):
    back = lax.axis_index("pipe") >= lax.axis_size("pipe") // 2
    own = pl.multiple_of(back.astype(jnp.int32) * middle, 128)
    return own, pl.multiple_of(middle - own, 128)


def select_kernel(*refs):
    far, near, sems, half_sems = refs[:4], refs[-6:-2], refs[-2], refs[-1]
    ids, gates, tokens, cotangent = near
    place_out, scale_out, *blocks = refs[4:-6]
    middle = blocks[0].shape[1]
    early = [pltpu.make_async_copy(far[i], near[i], sems.at[i]) for i in range(2)]
    halves = []
    for side, start in enumerate(halves_of(middle)):
        columns = pl.ds(start, middle)
        for which in range(2):
            source, target = far[2 + which].at[:, columns], near[2 + which].at[:, columns]
            halves.append(pltpu.make_async_copy(source, target, half_sems.at[side, which]))
    for copy in early + halves:
        copy.start()
    for copy in early:
        copy.wait()
    flight, count = len(blocks) // 2, ids.shape[1]
    slots = flight * CAP
    column = lax.broadcasted_iota(jnp.int32, (1, slots), 1)
    wanted = lax.axis_index("expert") // GROUP + column // CAP
    wanted = jnp.where(wanted >= flight, wanted - flight, wanted).astype(F32)
    named, weight = ids[...].astype(F32).T, gates[...].T
    hits, chosen = jnp.zeros((count, slots), F32), jnp.zeros((count, slots), F32)
    for choice in range(ids.shape[0]):
        match = (named[:, choice : choice + 1] == wanted).astype(F32)
        hits = hits + match
        chosen = chosen + match * weight[:, choice : choice + 1]
    row = lax.broadcasted_iota(jnp.int32, (count, count), 0)
    earlier = (lax.broadcasted_iota(jnp.int32, (count, count), 1) <= row).astype(BF16)
    slot = dot(earlier, hits.astype(BF16)) - 1.0
    level = (column % CAP).astype(F32)
    place = hits * (slot == level).astype(F32)
    place_bf = place.astype(BF16)
    place_out[...] = place_bf
    scale = lax.dot_general(
        place * chosen,
        jnp.ones((count, 128), F32),
        (((0,), (0,)), ((), ())),
        preferred_element_type=F32,
        precision=lax.Precision.HIGHEST,
    )
    scale_out[...] = scale
    for side, start in enumerate(halves_of(middle)):
        for copy in halves[2 * side : 2 * side + 2]:
            copy.wait()
        rows = dot(place_bf, tokens[:, pl.ds(start, middle)], (0, 0))
        scaled = dot(place_bf, cotangent[:, pl.ds(start, middle)], (0, 0)) * scale[:, :1]
        for step in range(flight):
            here = slice(step * CAP, (step + 1) * CAP)
            both = jnp.concatenate([rows[here], scaled[here]], axis=0)
            blocks[2 * step + side][...] = both.astype(BF16)


def pair_sum(own, other):
    blocks = [other[pl.ds((index ^ 1) * CAP, CAP), :] for index in range(other.shape[0] // CAP)]
    return own[...] + jnp.concatenate(blocks, axis=0)


def chunk_of(middle):
    return next(size for size in (512, 256, 128) if middle % size == 0)


def inner_kernel(*refs):
    pieces, (gate, up, down, slot_rows, scaled, inner) = refs[:-6], refs[-6:]
    row = 0
    for held in (pieces[:GROUP], pieces[GROUP:]):
        for unit in range(held[0].shape[0] // (4 * CAP)):
            for piece in held:
                here = pl.ds(row, 2 * CAP)
                slot_rows[here, :] = piece[pl.ds(unit * 4 * CAP, 2 * CAP), :]
                scaled[here, :] = piece[pl.ds((unit * 4 + 2) * CAP, 2 * CAP), :]
                row = row + 2 * CAP
    hidden_dim = gate.shape[2]
    both = jnp.concatenate([gate[0], up[0]], axis=1)
    inner[:, : 2 * hidden_dim] = dot(slot_rows[...], both)
    inner[:, 2 * hidden_dim :] = dot(scaled[...], down[0], (1, 1))


def return_kernel(first, own, other, gate, up, down, hidden_out, dinner_out, *parts):
    units = parts[0].shape[0] // (4 * CAP)
    rows = pl.ds(first * GROUP * 2 * CAP, units * GROUP * 2 * CAP)
    inner = pair_sum(own.at[rows, :], other.at[rows, :])
    hidden_dim = gate.shape[2]
    gate_pre, up_pre = inner[:, :hidden_dim], inner[:, hidden_dim : 2 * hidden_dim]
    dhidden = inner[:, 2 * hidden_dim :]
    sigma = jax.nn.sigmoid(gate_pre)
    active = gate_pre * sigma
    hidden = (active * up_pre).astype(BF16)
    dgate = (dhidden * up_pre * sigma * (1.0 + gate_pre * (1.0 - sigma))).astype(BF16)
    dup = (dhidden * active).astype(BF16)
    dinner = jnp.concatenate([dgate, dup], axis=1)
    hidden_out[...] = hidden
    dinner_out[...] = dinner
    middle = gate.shape[1]
    chunk = chunk_of(middle)

    @pl.loop(0, middle // chunk)
    def _(index):
        columns = pl.ds(pl.multiple_of(index * chunk, chunk), chunk)
        outs = dot(hidden, down[0, :, columns]).astype(BF16)
        both = jnp.concatenate([gate[0, columns, :], up[0, columns, :]], axis=1)
        dx = dot(dinner, both, (1, 1)).astype(BF16)
        for unit in range(units):
            for label, part in enumerate(parts):
                here = slice((unit * GROUP + label) * 2 * CAP, (unit * GROUP + label + 1) * 2 * CAP)
                part[pl.ds(unit * 4 * CAP, 2 * CAP), columns] = outs[here]
                part[pl.ds((unit * 4 + 2) * CAP, 2 * CAP), columns] = dx[here]


def grad_kernel(slot_rows, scaled, near_hidden, near_dinner, far_hidden, far_dinner, *refs):
    far, done, near, sems = refs[:3], refs[3], refs[4:7], refs[7]
    done[...] = jnp.zeros_like(done)
    hidden = jnp.concatenate([near_hidden[...], far_hidden[...]], axis=0)
    dinner = jnp.concatenate([near_dinner[...], far_dinner[...]], axis=0)
    middle, hidden_dim = slot_rows.shape[1], hidden.shape[1]
    chunk = chunk_of(middle)
    copies = []
    for index in range(middle // chunk):
        columns = pl.ds(index * chunk, chunk)
        value = dot(slot_rows[:, columns], dinner, (0, 0)).astype(BF16)
        near[0][0, columns, :] = value[:, :hidden_dim]
        near[1][0, columns, :] = value[:, hidden_dim:]
        near[2][0, :, columns] = dot(hidden, scaled[:, columns], (0, 0)).astype(BF16)
        places = [(0, columns), (0, columns), (0, slice(None), columns)]
        for which, at in enumerate(places):
            copies.append(
                pltpu.make_async_copy(near[which].at[at], far[which].at[at], sems.at[which, index])
            )
            copies[-1].start()
    for copy in copies:
        copy.wait()


def merge_kernel(place, scale, *refs):
    outs, nears, sems = refs[-5:-3], refs[-3:-1], refs[-1]
    blocks = refs[:-5]
    middle, parts = blocks[0].shape[1], sems.shape[2]
    chunk = middle // parts
    copies = []
    for side, start in enumerate(halves_of(middle)):
        for part in range(parts):
            here = pl.ds(part * chunk, chunk)
            held = [block[:, here].astype(F32) for block in blocks[side::2]]
            columns = pl.ds(pl.multiple_of(start + part * chunk, 128), chunk)
            for which, (out, near) in enumerate(zip(outs, nears)):
                rows = [value[which * CAP : (which + 1) * CAP] for value in held]
                rows = jnp.concatenate(rows, axis=0)
                if which == 0:
                    rows = rows * scale[:, :1]
                near[:, columns] = dot(place[...], rows.astype(BF16)).astype(BF16)
                sem = sems.at[which, side, part]
                copies.append(pltpu.make_async_copy(near.at[:, columns], out.at[:, columns], sem))
                copies[-1].start()
    for copy in copies:
        copy.wait()


def per_device(tokens, cotangent, expert_ids, gate_weights, w_gate, w_up, w_down):
    flight = lax.axis_size("expert") // GROUP
    tok_count, width = tokens.shape
    middle, hidden_dim = w_gate.shape[1], w_gate.shape[2]
    slots = flight * CAP
    near_rows, far_rows = GROUP * 2 * CAP, (flight - 1) * GROUP * 2 * CAP
    count = near_rows + far_rows
    pair, whole = ((2 * CAP, middle), BF16), ((count, middle), BF16)
    unit, units = ((4 * CAP, middle), BF16), ((4 * CAP * (flight - 1), middle), BF16)
    result, token = ((tok_count, width), BF16), ((8, 128), F32)
    weights = [w_gate, w_up, w_down]
    done, open_steps = {}, set()

    def get(name):
        if name not in done:
            if name in open_steps:
                raise ValueError(name)
            open_steps.add(name)
            done[name] = steps[name](name)
        return done[name]

    def run(name, kernel, shapes, operands, **options):
        after = [get(other)[-1] for other in AFTER.get(name, ())]
        return call(kernel, shapes, operands, after=after, cost=COST.get(name, 1), **options)

    def sent(name, block, bit):
        if AFTER.get(name):
            block = run(name, copy_kernel, [(block.shape, BF16)], [block])[0]
        return [neighbour(block, bit)]

    def spread_step(name):
        tree, label = name[0], int(name[1:])
        before, bit = TREES[tree][label]
        return sent(name, get(tree + str(before))[0], bit)

    def reduce_step(name):
        tree, label = name[0], int(name[1:])
        total = summands(tree, label)
        if len(total) > 1:
            total = run(name, add_kernel, [(total[0].shape, BF16)], total)
            return [neighbour(total[0], TREES[tree][label][1])]
        return sent(name, total[0], TREES[tree][label][1])

    def summands(tree, label):
        arrived = [key for key, (before, _) in TREES[tree].items() if before == label]
        return [get(tree)[label]] + [get(tree + str(key))[0] for key in arrived]

    def summed(name, tree, number):
        blocks = summands(tree, 0)
        kernel = functools.partial(split_sum_kernel, len(blocks) - 1)
        return run(name, kernel, [pair] * number, blocks)

    def select(name):
        operands = [expert_ids.T, gate_weights.T, tokens, cotangent]
        return run(
            name,
            select_kernel,
            [((tok_count, slots), BF16), ((slots, 128), F32)] + [pair] * (2 * flight),
            operands,
            far=range(4),
            scratch=[pltpu.VMEM(x.shape, x.dtype) for x in operands]
            + [pltpu.SemaphoreType.DMA((2,)), pltpu.SemaphoreType.DMA((2, 2))],
            limit=52 * 1024 * 1024,
        )

    def far_there(name):
        blocks = get("select")[2:]
        parts = []
        for step in range(1, flight):
            parts.append(moved(blocks[2 * step], False, step))
            parts.append(moved(blocks[2 * step + 1], True, step))
        return parts

    def far_back(name):
        blocks = summed(name, "C", 2 * (flight - 1))
        parts = []
        for step in range(1, flight):
            parts.append(moved(blocks[2 * step - 2], False, flight - step))
            parts.append(moved(blocks[2 * step - 1], True, flight - step))
        return parts

    def near_back(name):
        own, other = summed(name, "D", 2)
        return [own, moved(other, True, 0)]

    def inner(name):
        pieces = [get(tree + str(label))[0] for tree in "AB" for label in range(GROUP)]
        shapes = [whole, whole, ((count, 3 * hidden_dim), F32)]
        return run(name, inner_kernel, shapes, pieces + weights)

    def returned(name, first, rows, shape):
        partial = get("inner")[2]
        results = run(
            name,
            functools.partial(return_kernel, first),
            [((rows, hidden_dim), BF16), ((rows, 2 * hidden_dim), BF16)] + [shape] * GROUP,
            [partial, get("inner_other")[0]] + weights,
        )
        return results[2:] + results[:2]

    def grads(name):
        shapes = [w_gate.shape, w_up.shape, w_down.shape]
        return run(
            name,
            grad_kernel,
            [(shape, BF16) for shape in shapes] + [token],
            get("inner")[:2] + get("D")[GROUP:] + get("C")[GROUP:],
            far_out=3,
            scratch=[pltpu.VMEM(shape, BF16) for shape in shapes]
            + [pltpu.SemaphoreType.DMA((3, middle // chunk_of(middle)))],
        )

    def merged(name):
        parts = 4 if middle % 512 == 0 else 1
        return run(
            name,
            merge_kernel,
            [result] * 2,
            get("select")[:2] + get("near_back") + get("far_back"),
            far_out=2,
            scratch=[pltpu.VMEM((tok_count, width), BF16)] * 2
            + [pltpu.SemaphoreType.DMA((2, 2, parts))],
        )

    steps = {
        "select": select,
        "near_there": lambda name: [moved(get("select")[3], True, 0)],
        "far_there": far_there,
        "A0": lambda name: run(name, join_kernel, [unit], [get("select")[2]] + get("near_there")),
        "B0": lambda name: run(name, join_kernel, [units], get("far_there")),
        "inner": inner,
        "inner_other": lambda name: [moved(get("inner")[2], True, 0)],
        "C": lambda name: returned(name, 1, far_rows, units),
        "D": lambda name: returned(name, 0, near_rows, unit),
        "grads": grads,
        "far_back": far_back,
        "near_back": near_back,
        "merged": merged,
    }
    for label in TREES["A"]:
        steps["A" + str(label)] = steps["B" + str(label)] = spread_step
        steps["C" + str(label)] = steps["D" + str(label)] = reduce_step
    grad_gate, grad_up, grad_down, _ = get("grads")
    mixed_out, input_grad = get("merged")
    return mixed_out, input_grad, grad_gate, grad_up, grad_down


def solution(mesh):
    rows = P(("pipe", "expert"), None)
    columns = P("pipe", None, "expert")
    downs = P("pipe", "expert", None)
    return jax.shard_map(
        per_device,
        mesh=mesh,
        in_specs=(rows, rows, rows, rows, columns, columns, downs),
        out_specs=(rows, rows, columns, columns, downs),
        check_vma=False,
    )
```

```python
import functools

import jax
import jax.numpy as jnp
from jax import lax
from jax.experimental import pallas as pl
from jax.experimental.pallas import tpu as pltpu
from jax.sharding import PartitionSpec as P

GROUP = 8
CAP = 8
BF16, F32 = jnp.bfloat16, jnp.float32
AXES = ("pipe", "expert")
VMEM = pl.BlockSpec(memory_space=pltpu.VMEM)
ANY = pl.BlockSpec(memory_space=pl.ANY)
LIMIT = 16 * 1024 * 1024


TREES = {
    "A": {4: (0, 2), 1: (0, 0), 2: (0, 1), 3: (2, 0), 5: (1, 2), 6: (4, 1), 7: (5, 1)},
    "B": {1: (0, 0), 4: (0, 2), 2: (0, 1), 6: (4, 1), 5: (1, 2), 3: (2, 0), 7: (6, 0)},
    "C": {4: (0, 2), 1: (0, 0), 2: (0, 1), 5: (4, 0), 6: (4, 1), 3: (1, 1), 7: (3, 2)},
    "D": {4: (0, 2), 2: (0, 1), 1: (0, 0), 6: (2, 2), 3: (2, 0), 5: (4, 0), 7: (3, 2)},
}

AFTER = {
    "D4": ["C4"],
    "D1": ["D3", "D7"],
    "B0": ["A5", "A6", "A3"],
    "grads": ["D6", "C5"],
    "C": ["B5", "B3"],
    "inner": ["B6"],
    "C6": ["inner_other"],
    "D6": ["C5"],
    "A2": ["near_there"],
    "merged": ["D5", "far_back"],
    "A6": ["A3"],
    "A5": ["A4"],
    "far_back": ["C6"],
    "B7": ["B4"],
    "A3": ["far_there"],
}

ORDER = []

COST = {"merged": 20000000, "A0": 4000000, "near_back": 20000000, "select": 4000000, "C": 1000000, "B0": 1000000, "D": 1000000}


def moved(block, mirror, step):
    ranks, owners = lax.axis_size("pipe"), lax.axis_size("expert")
    route = []
    for rank in range(ranks):
        target = ranks - 1 - rank if mirror else rank
        for index in range(owners):
            route.append((rank * owners + index, target * owners + (index + step * GROUP) % owners))
    return lax.ppermute(block, AXES, route)


def neighbour(block, bit):
    owners = lax.axis_size("expert")
    return lax.ppermute(block, "expert", [(index, index ^ 1 << bit) for index in range(owners)])


def dot(a, b, contract=(1, 0)):
    return lax.dot_general(
        a, b, (((contract[0],), (contract[1],)), ((), ())), preferred_element_type=F32
    )


def call(kernel, shapes, operands, after=(), far=(), far_out=0, scratch=(), cost=1, alias=None, limit=LIMIT):
    out = [jax.ShapeDtypeStruct(shape, dtype) for shape, dtype in shapes]
    count = len(operands)
    specs = [ANY if i in far else VMEM for i in range(count)]

    def body(*refs):
        kernel(*refs[:count], *refs[count + len(after) :])

    results = pl.pallas_call(
        body,
        out_shape=out,
        in_specs=specs + [ANY] * len(after),
        out_specs=[ANY if i < far_out else VMEM for i in range(len(out))],
        scratch_shapes=list(scratch),
        input_output_aliases=alias or {},
        compiler_params=pltpu.CompilerParams(vmem_limit_bytes=limit),
        cost_estimate=pl.CostEstimate(flops=1, bytes_accessed=cost, transcendentals=0),
    )(*operands, *after)
    return list(results)


def copy_kernel(block, out):
    out[...] = block[...]


def add_kernel(*refs):
    total = refs[0][...].astype(F32)
    for ref in refs[1:-1]:
        total = total + ref[...].astype(F32)
    refs[-1][...] = total.astype(BF16)


def join_kernel(own, other, *units):
    for step, out in enumerate(units):
        here = pl.ds(step * 2 * CAP, 2 * CAP)
        mine, theirs = own[here, :].astype(F32), other[here, :].astype(F32)
        unit = jnp.concatenate([mine[:CAP], theirs[:CAP], mine[CAP:], theirs[CAP:]], axis=0)
        out[...] = unit.astype(BF16)


def stack_kernel(*refs):
    rows = refs[0].shape[0]
    for index, ref in enumerate(refs[:-1]):
        refs[-1][pl.ds(index * rows, rows), :] = ref[...]


def split_sum_kernel(arrived, *refs):
    blocks, pieces = refs[: arrived + 1], refs[arrived + 1 :]
    for index in range(0, len(pieces), 2):
        rows = pl.ds(index * 2 * CAP, 4 * CAP)
        unit = blocks[0][rows, :].astype(F32)
        for block in blocks[1:]:
            unit = unit + block[rows, :].astype(F32)
        parts = [unit[place * CAP : (place + 1) * CAP] for place in range(4)]
        pieces[index][...] = jnp.concatenate(parts[0::2], axis=0).astype(BF16)
        pieces[index + 1][...] = jnp.concatenate(parts[1::2], axis=0).astype(BF16)


def halves_of(middle):
    back = lax.axis_index("pipe") >= lax.axis_size("pipe") // 2
    own = pl.multiple_of(back.astype(jnp.int32) * middle, 128)
    return own, pl.multiple_of(middle - own, 128)


def select_kernel(*refs):
    far, near, sems, half_sems = refs[:4], refs[-6:-2], refs[-2], refs[-1]
    ids, gates, tokens, cotangent = near
    place_out, scale_out, *blocks = refs[4:-6]
    middle = blocks[0].shape[1]
    early = [pltpu.make_async_copy(far[i], near[i], sems.at[i]) for i in range(2)]
    halves = []
    for side, start in enumerate(halves_of(middle)):
        columns = pl.ds(start, middle)
        for which in range(2):
            source, target = far[2 + which].at[:, columns], near[2 + which].at[:, columns]
            halves.append(pltpu.make_async_copy(source, target, half_sems.at[side, which]))
    for copy in early + halves:
        copy.start()
    for copy in early:
        copy.wait()
    flight, count = blocks[0].shape[0] // (2 * CAP), ids.shape[1]
    slots = flight * CAP
    column = lax.broadcasted_iota(jnp.int32, (1, slots), 1)
    wanted = lax.axis_index("expert") // GROUP + column // CAP
    wanted = jnp.where(wanted >= flight, wanted - flight, wanted).astype(F32)
    named, weight = ids[...].astype(F32).T, gates[...].T
    hits, chosen = jnp.zeros((count, slots), F32), jnp.zeros((count, slots), F32)
    for choice in range(ids.shape[0]):
        match = (named[:, choice : choice + 1] == wanted).astype(F32)
        hits = hits + match
        chosen = chosen + match * weight[:, choice : choice + 1]
    row = lax.broadcasted_iota(jnp.int32, (count, count), 0)
    earlier = (lax.broadcasted_iota(jnp.int32, (count, count), 1) <= row).astype(BF16)
    slot = dot(earlier, hits.astype(BF16)) - 1.0
    level = (column % CAP).astype(F32)
    place = hits * (slot == level).astype(F32)
    place_bf = place.astype(BF16)
    place_out[...] = place_bf
    scale = lax.dot_general(
        place * chosen,
        jnp.ones((count, 128), F32),
        (((0,), (0,)), ((), ())),
        preferred_element_type=F32,
        precision=lax.Precision.HIGHEST,
    )
    scale_out[...] = scale
    for side, start in enumerate(halves_of(middle)):
        for copy in halves[2 * side : 2 * side + 2]:
            copy.wait()
        rows = dot(place_bf, tokens[:, pl.ds(start, middle)], (0, 0))
        scaled = dot(place_bf, cotangent[:, pl.ds(start, middle)], (0, 0)) * scale[:, :1]
        parts = []
        for step in range(flight):
            here = slice(step * CAP, (step + 1) * CAP)
            parts = parts + [rows[here], scaled[here]]
        blocks[side][...] = jnp.concatenate(parts, axis=0).astype(BF16)


def pair_sum(own, other):
    blocks = [other[pl.ds((index ^ 1) * CAP, CAP), :] for index in range(other.shape[0] // CAP)]
    return own[...] + jnp.concatenate(blocks, axis=0)


def chunk_of(middle):
    return next(size for size in (512, 256, 128) if middle % size == 0)


def inner_kernel(*refs):
    pieces, (gate, up, down, slot_rows, scaled, inner) = refs[:-6], refs[-6:]
    row = 0
    for held in (pieces[:GROUP], pieces[GROUP:]):
        for unit in range(held[0].shape[0] // (4 * CAP)):
            for piece in held:
                here = pl.ds(row, 2 * CAP)
                slot_rows[here, :] = piece[pl.ds(unit * 4 * CAP, 2 * CAP), :]
                scaled[here, :] = piece[pl.ds((unit * 4 + 2) * CAP, 2 * CAP), :]
                row = row + 2 * CAP
    hidden_dim = gate.shape[2]
    both = jnp.concatenate([gate[0], up[0]], axis=1)
    inner[:, : 2 * hidden_dim] = dot(slot_rows[...], both)
    inner[:, 2 * hidden_dim :] = dot(scaled[...], down[0], (1, 1))


def return_kernel(first, own, other, gate, up, down, hidden_out, dinner_out, *parts):
    units = parts[0].shape[0] // (4 * CAP)
    rows = pl.ds(first * GROUP * 2 * CAP, units * GROUP * 2 * CAP)
    inner = pair_sum(own.at[rows, :], other.at[rows, :])
    hidden_dim = gate.shape[2]
    gate_pre, up_pre = inner[:, :hidden_dim], inner[:, hidden_dim : 2 * hidden_dim]
    dhidden = inner[:, 2 * hidden_dim :]
    sigma = jax.nn.sigmoid(gate_pre)
    active = gate_pre * sigma
    hidden = (active * up_pre).astype(BF16)
    dgate = (dhidden * up_pre * sigma * (1.0 + gate_pre * (1.0 - sigma))).astype(BF16)
    dup = (dhidden * active).astype(BF16)
    dinner = jnp.concatenate([dgate, dup], axis=1)
    hidden_out[...] = hidden
    dinner_out[...] = dinner
    middle = gate.shape[1]
    chunk = chunk_of(middle)

    @pl.loop(0, middle // chunk)
    def _(index):
        columns = pl.ds(pl.multiple_of(index * chunk, chunk), chunk)
        outs = dot(hidden, down[0, :, columns]).astype(BF16)
        both = jnp.concatenate([gate[0, columns, :], up[0, columns, :]], axis=1)
        dx = dot(dinner, both, (1, 1)).astype(BF16)
        for unit in range(units):
            for label, part in enumerate(parts):
                here = slice((unit * GROUP + label) * 2 * CAP, (unit * GROUP + label + 1) * 2 * CAP)
                part[pl.ds(unit * 4 * CAP, 2 * CAP), columns] = outs[here]
                part[pl.ds((unit * 4 + 2) * CAP, 2 * CAP), columns] = dx[here]


def grad_kernel(slot_rows, scaled, near_hidden, near_dinner, far_hidden, far_dinner, *refs):
    far, done, near, sems = refs[:3], refs[3], refs[4:7], refs[7]
    done[...] = jnp.zeros_like(done)
    hidden = jnp.concatenate([near_hidden[...], far_hidden[...]], axis=0)
    dinner = jnp.concatenate([near_dinner[...], far_dinner[...]], axis=0)
    middle, hidden_dim = slot_rows.shape[1], hidden.shape[1]
    chunk = chunk_of(middle)
    copies = []
    for index in range(middle // chunk):
        columns = pl.ds(index * chunk, chunk)
        value = dot(slot_rows[:, columns], dinner, (0, 0)).astype(BF16)
        near[0][0, columns, :] = value[:, :hidden_dim]
        near[1][0, columns, :] = value[:, hidden_dim:]
        near[2][0, :, columns] = dot(hidden, scaled[:, columns], (0, 0)).astype(BF16)
        places = [(0, columns), (0, columns), (0, slice(None), columns)]
        for which, at in enumerate(places):
            copies.append(
                pltpu.make_async_copy(near[which].at[at], far[which].at[at], sems.at[which, index])
            )
            copies[-1].start()
    for copy in copies:
        copy.wait()


def merge_kernel(place, scale, *refs):
    outs, nears, sems = refs[-5:-3], refs[-3:-1], refs[-1]
    blocks = refs[:-5]
    middle, parts = blocks[0].shape[1], sems.shape[2]
    chunk = middle // parts
    copies = []
    for side, start in enumerate(halves_of(middle)):
        for part in range(parts):
            here = pl.ds(part * chunk, chunk)
            held = [block[:, here].astype(F32) for block in blocks[side::2]]
            columns = pl.ds(pl.multiple_of(start + part * chunk, 128), chunk)
            for which, (out, near) in enumerate(zip(outs, nears)):
                rows = [value[which * CAP : (which + 1) * CAP] for value in held]
                rows = jnp.concatenate(rows, axis=0)
                if which == 0:
                    rows = rows * scale[:, :1]
                near[:, columns] = dot(place[...], rows.astype(BF16)).astype(BF16)
                sem = sems.at[which, side, part]
                copies.append(pltpu.make_async_copy(near.at[:, columns], out.at[:, columns], sem))
                copies[-1].start()
    for copy in copies:
        copy.wait()


def per_device(tokens, cotangent, expert_ids, gate_weights, w_gate, w_up, w_down):
    flight = lax.axis_size("expert") // GROUP
    tok_count, width = tokens.shape
    middle, hidden_dim = w_gate.shape[1], w_gate.shape[2]
    slots = flight * CAP
    near_rows, far_rows = GROUP * 2 * CAP, (flight - 1) * GROUP * 2 * CAP
    count = near_rows + far_rows
    pair, whole = ((2 * CAP, middle), BF16), ((count, middle), BF16)
    unit, units_shape = ((4 * CAP, middle), BF16), ((4 * CAP * (flight - 1), middle), BF16)
    both = ((2 * CAP * flight, middle), BF16)
    result, token = ((tok_count, width), BF16), ((8, 128), F32)
    weights = [w_gate, w_up, w_down]
    done, open_steps = {}, set()

    def get(name):
        if name not in done:
            if name in open_steps:
                raise ValueError(name)
            open_steps.add(name)
            done[name] = steps[name](name)
        return done[name]

    def run(name, kernel, shapes, operands, **options):
        after = [get(other)[-1] for other in AFTER.get(name, ())]
        return call(kernel, shapes, operands, after=after, cost=COST.get(name, 1), **options)

    def sent(name, block, bit):
        if AFTER.get(name):
            block = run(name, copy_kernel, [(block.shape, BF16)], [block])[0]
        return [neighbour(block, bit)]

    def spread_step(name):
        tree, label = name[0], int(name[1:])
        before, bit = TREES[tree][label]
        return sent(name, get(tree + str(before))[0], bit)

    def reduce_step(name):
        tree, label = name[0], int(name[1:])
        total = summands(tree, label)
        if len(total) > 1:
            total = run(name, add_kernel, [(total[0].shape, BF16)], total)
            return [neighbour(total[0], TREES[tree][label][1])]
        return sent(name, total[0], TREES[tree][label][1])

    def summands(tree, label):
        arrived = [key for key, (before, _) in TREES[tree].items() if before == label]
        return [get(tree)[label]] + [get(tree + str(key))[0] for key in arrived]

    def summed(name, tree, number):
        blocks = summands(tree, 0)
        kernel = functools.partial(split_sum_kernel, len(blocks) - 1)
        return run(name, kernel, [pair] * number, blocks)

    def select(name):
        operands = [expert_ids.T, gate_weights.T, tokens, cotangent]
        return run(
            name,
            select_kernel,
            [((tok_count, slots), BF16), ((slots, 128), F32)] + [both] * 2,
            operands,
            far=range(4),
            scratch=[pltpu.VMEM(x.shape, x.dtype) for x in operands]
            + [pltpu.SemaphoreType.DMA((2,)), pltpu.SemaphoreType.DMA((2, 2))],
            limit=52 * 1024 * 1024,
        )

    def far_unit(name):
        units = get("far_there")
        return units if flight == 2 else run(name, stack_kernel, [units_shape], units)

    def far_back(name):
        blocks = summed(name, "C", 2 * (flight - 1))
        parts = []
        for step in range(1, flight):
            parts.append(moved(blocks[2 * step - 2], False, flight - step))
            parts.append(moved(blocks[2 * step - 1], True, flight - step))
        return parts

    def near_back(name):
        own, other = summed(name, "D", 2)
        return [own, moved(other, True, 0)]

    def inner(name):
        pieces = [get(tree + str(label))[0] for tree in "AB" for label in range(GROUP)]
        shapes = [whole, whole, ((count, 3 * hidden_dim), F32)]
        return run(name, inner_kernel, shapes, pieces + weights)

    def returned(name, first, rows, shape):
        partial = get("inner")[2]
        results = run(
            name,
            functools.partial(return_kernel, first),
            [((rows, hidden_dim), BF16), ((rows, 2 * hidden_dim), BF16)] + [shape] * GROUP,
            [partial, get("inner_other")[0]] + weights,
        )
        return results[2:] + results[:2]

    def grads(name):
        shapes = [w_gate.shape, w_up.shape, w_down.shape]
        return run(
            name,
            grad_kernel,
            [(shape, BF16) for shape in shapes] + [token],
            get("inner")[:2] + get("D")[GROUP:] + get("C")[GROUP:],
            far_out=3,
            scratch=[pltpu.VMEM(shape, BF16) for shape in shapes]
            + [pltpu.SemaphoreType.DMA((3, middle // chunk_of(middle)))],
        )

    def merged(name):
        parts = 4 if middle % 512 == 0 else 1
        return run(
            name,
            merge_kernel,
            [result] * 2,
            get("select")[:2] + get("near_back") + get("far_back"),
            far_out=2,
            scratch=[pltpu.VMEM((tok_count, width), BF16)] * 2
            + [pltpu.SemaphoreType.DMA((2, 2, parts))],
        )

    steps = {
        "select": select,
        "near_there": lambda name: [moved(get("select")[3], True, 0)],
        "A0": lambda name: run(
            name, join_kernel, [unit] * flight, [get("select")[2]] + get("near_there")
        ),
        "far_there": lambda name: [
            moved(get("A0")[step], False, step) for step in range(1, flight)
        ],
        "B0": far_unit,
        "inner": inner,
        "inner_other": lambda name: [moved(get("inner")[2], True, 0)],
        "C": lambda name: returned(name, 1, far_rows, units_shape),
        "D": lambda name: returned(name, 0, near_rows, unit),
        "grads": grads,
        "far_back": far_back,
        "near_back": near_back,
        "merged": merged,
    }
    for label in TREES["A"]:
        steps["A" + str(label)] = steps["B" + str(label)] = spread_step
        steps["C" + str(label)] = steps["D" + str(label)] = reduce_step
    for name in ORDER:
        get(name)
    grad_gate, grad_up, grad_down, _ = get("grads")
    mixed_out, input_grad = get("merged")
    return mixed_out, input_grad, grad_gate, grad_up, grad_down


def solution(mesh):
    rows = P(("pipe", "expert"), None)
    columns = P("pipe", None, "expert")
    downs = P("pipe", "expert", None)
    return jax.shard_map(
        per_device,
        mesh=mesh,
        in_specs=(rows, rows, rows, rows, columns, columns, downs),
        out_specs=(rows, rows, columns, columns, downs),
        check_vma=False,
    )
```

```python
import functools

import jax
import jax.numpy as jnp
from jax import lax
from jax.experimental import pallas as pl
from jax.experimental.pallas import tpu as pltpu
from jax.sharding import PartitionSpec as P

GROUP = 8
CAP = 8
BF16, F32 = jnp.bfloat16, jnp.float32
AXES = ("pipe", "expert")
VMEM = pl.BlockSpec(memory_space=pltpu.VMEM)
ANY = pl.BlockSpec(memory_space=pl.ANY)
LIMIT = 16 * 1024 * 1024


TREES = {
    "A": {4: (0, 2), 1: (0, 0), 2: (0, 1), 3: (2, 0), 5: (1, 2), 6: (4, 1), 7: (5, 1)},
    "B": {1: (0, 0), 4: (0, 2), 2: (0, 1), 6: (4, 1), 5: (1, 2), 3: (2, 0), 7: (6, 0)},
    "C": {4: (0, 2), 1: (0, 0), 2: (0, 1), 5: (4, 0), 6: (4, 1), 3: (1, 1), 7: (3, 2)},
    "D": {4: (0, 2), 2: (0, 1), 1: (0, 0), 6: (2, 2), 3: (2, 0), 5: (4, 0), 7: (3, 2)},
}

AFTER = {
    "D4": ["C4"],
    "D1": ["D3", "D7"],
    "B0": ["A5", "A6", "A3"],
    "grads": ["D6", "C5"],
    "C": ["B5", "B3", "inner_other"],
    "inner": ["B6"],
    "C6": ["inner_other"],
    "D6": ["C5"],
    "A2": ["near_there"],
    "merged": ["D5", "far_back"],
    "A6": ["A3"],
    "A5": ["A4"],
    "B7": ["B4"],
    "A3": ["far_there"],
    "C4": ["inner_other"],
    "D7": ["A4"],
}

ORDER = []

COST = {"merged": 20000000, "A0": 4000000, "near_back": 20000000, "select": 4000000, "B0": 1000000, "D": 1000000}


def moved(block, mirror, step):
    ranks, owners = lax.axis_size("pipe"), lax.axis_size("expert")
    route = []
    for rank in range(ranks):
        target = ranks - 1 - rank if mirror else rank
        for index in range(owners):
            route.append((rank * owners + index, target * owners + (index + step * GROUP) % owners))
    return lax.ppermute(block, AXES, route)


def neighbour(block, bit):
    owners = lax.axis_size("expert")
    return lax.ppermute(block, "expert", [(index, index ^ 1 << bit) for index in range(owners)])


def dot(a, b, contract=(1, 0)):
    return lax.dot_general(
        a, b, (((contract[0],), (contract[1],)), ((), ())), preferred_element_type=F32
    )


def call(kernel, shapes, operands, after=(), far=(), far_out=0, scratch=(), cost=1, alias=None, limit=LIMIT):
    out = [jax.ShapeDtypeStruct(shape, dtype) for shape, dtype in shapes]
    count = len(operands)
    specs = [ANY if i in far else VMEM for i in range(count)]

    def body(*refs):
        kernel(*refs[:count], *refs[count + len(after) :])

    results = pl.pallas_call(
        body,
        out_shape=out,
        in_specs=specs + [ANY] * len(after),
        out_specs=[ANY if i < far_out else VMEM for i in range(len(out))],
        scratch_shapes=list(scratch),
        input_output_aliases=alias or {},
        compiler_params=pltpu.CompilerParams(vmem_limit_bytes=limit),
        cost_estimate=pl.CostEstimate(flops=1, bytes_accessed=cost, transcendentals=0),
    )(*operands, *after)
    return list(results)


def copy_kernel(block, out):
    out[...] = block[...]


def add_kernel(*refs):
    total = refs[0][...].astype(F32)
    for ref in refs[1:-1]:
        total = total + ref[...].astype(F32)
    refs[-1][...] = total.astype(BF16)


def join_kernel(own, other, *units):
    for step, out in enumerate(units):
        here = pl.ds(step * 2 * CAP, 2 * CAP)
        mine, theirs = own[here, :].astype(F32), other[here, :].astype(F32)
        unit = jnp.concatenate([mine[:CAP], theirs[:CAP], mine[CAP:], theirs[CAP:]], axis=0)
        out[...] = unit.astype(BF16)


def stack_kernel(*refs):
    rows = refs[0].shape[0]
    for index, ref in enumerate(refs[:-1]):
        refs[-1][pl.ds(index * rows, rows), :] = ref[...]


def split_sum_kernel(arrived, *refs):
    blocks, pieces = refs[: arrived + 1], refs[arrived + 1 :]
    for index in range(0, len(pieces), 2):
        rows = pl.ds(index * 2 * CAP, 4 * CAP)
        unit = blocks[0][rows, :].astype(F32)
        for block in blocks[1:]:
            unit = unit + block[rows, :].astype(F32)
        parts = [unit[place * CAP : (place + 1) * CAP] for place in range(4)]
        pieces[index][...] = jnp.concatenate(parts[0::2], axis=0).astype(BF16)
        pieces[index + 1][...] = jnp.concatenate(parts[1::2], axis=0).astype(BF16)


def halves_of(middle):
    back = lax.axis_index("pipe") >= lax.axis_size("pipe") // 2
    own = pl.multiple_of(back.astype(jnp.int32) * middle, 128)
    return own, pl.multiple_of(middle - own, 128)


def select_kernel(*refs):
    choices, far, place_out, scale_out, blocks = refs[0], refs[1:3], refs[3], refs[4], refs[5:-3]
    tokens, cotangent, sems = refs[-3:]
    middle = blocks[0].shape[1]
    copies = []
    for side, start in enumerate(halves_of(middle)):
        columns = pl.ds(start, middle)
        for which, near in enumerate((tokens, cotangent)):
            source, target = far[which].at[:, columns], near.at[:, columns]
            copies.append(pltpu.make_async_copy(source, target, sems.at[side, which]))
            copies[-1].start()
    flight, count, top = blocks[0].shape[0] // (2 * CAP), choices.shape[2], choices.shape[1]
    slots = flight * CAP
    column = lax.broadcasted_iota(jnp.int32, (1, slots), 1)
    wanted = lax.axis_index("expert") // GROUP + column // CAP
    wanted = jnp.where(wanted >= flight, wanted - flight, wanted).astype(F32)
    named, weight = choices[0].T, choices[1].T
    hits, chosen = jnp.zeros((count, slots), F32), jnp.zeros((count, slots), F32)
    for choice in range(top):
        match = (named[:, choice : choice + 1] == wanted).astype(F32)
        hits = hits + match
        chosen = chosen + match * weight[:, choice : choice + 1]
    row = lax.broadcasted_iota(jnp.int32, (count, count), 0)
    earlier = (lax.broadcasted_iota(jnp.int32, (count, count), 1) <= row).astype(BF16)
    slot = dot(earlier, hits.astype(BF16)) - 1.0
    level = (column % CAP).astype(F32)
    place = hits * (slot == level).astype(F32)
    place_bf = place.astype(BF16)
    place_out[...] = place_bf
    scale = lax.dot_general(
        place * chosen,
        jnp.ones((count, 128), F32),
        (((0,), (0,)), ((), ())),
        preferred_element_type=F32,
        precision=lax.Precision.HIGHEST,
    )
    scale_out[...] = scale
    for side, start in enumerate(halves_of(middle)):
        for copy in copies[2 * side : 2 * side + 2]:
            copy.wait()
        rows = dot(place_bf, tokens[:, pl.ds(start, middle)], (0, 0))
        scaled = dot(place_bf, cotangent[:, pl.ds(start, middle)], (0, 0)) * scale[:, :1]
        parts = []
        for step in range(flight):
            here = slice(step * CAP, (step + 1) * CAP)
            parts = parts + [rows[here], scaled[here]]
        blocks[side][...] = jnp.concatenate(parts, axis=0).astype(BF16)


def pair_sum(own, other):
    blocks = [other[pl.ds((index ^ 1) * CAP, CAP), :] for index in range(other.shape[0] // CAP)]
    return own[...] + jnp.concatenate(blocks, axis=0)


def chunk_of(middle):
    return next(size for size in (512, 256, 128) if middle % size == 0)


def inner_kernel(*refs):
    pieces, (gate, up, down, slot_rows, scaled, inner) = refs[:-6], refs[-6:]
    row = 0
    for held in (pieces[:GROUP], pieces[GROUP:]):
        for unit in range(held[0].shape[0] // (4 * CAP)):
            for piece in held:
                here = pl.ds(row, 2 * CAP)
                slot_rows[here, :] = piece[pl.ds(unit * 4 * CAP, 2 * CAP), :]
                scaled[here, :] = piece[pl.ds((unit * 4 + 2) * CAP, 2 * CAP), :]
                row = row + 2 * CAP
    hidden_dim = gate.shape[2]
    both = jnp.concatenate([gate[0], up[0]], axis=1)
    inner[:, : 2 * hidden_dim] = dot(slot_rows[...], both)
    inner[:, 2 * hidden_dim :] = dot(scaled[...], down[0], (1, 1))


def return_kernel(first, own, other, gate, up, down, hidden_out, dinner_out, *parts):
    units = parts[0].shape[0] // (4 * CAP)
    rows = pl.ds(first * GROUP * 2 * CAP, units * GROUP * 2 * CAP)
    inner = pair_sum(own.at[rows, :], other.at[rows, :])
    hidden_dim = gate.shape[2]
    gate_pre, up_pre = inner[:, :hidden_dim], inner[:, hidden_dim : 2 * hidden_dim]
    dhidden = inner[:, 2 * hidden_dim :]
    sigma = jax.nn.sigmoid(gate_pre)
    active = gate_pre * sigma
    hidden = (active * up_pre).astype(BF16)
    dgate = (dhidden * up_pre * sigma * (1.0 + gate_pre * (1.0 - sigma))).astype(BF16)
    dup = (dhidden * active).astype(BF16)
    dinner = jnp.concatenate([dgate, dup], axis=1)
    hidden_out[...] = hidden
    dinner_out[...] = dinner
    middle = gate.shape[1]
    chunk = chunk_of(middle)

    @pl.loop(0, middle // chunk)
    def _(index):
        columns = pl.ds(pl.multiple_of(index * chunk, chunk), chunk)
        outs = dot(hidden, down[0, :, columns]).astype(BF16)
        both = jnp.concatenate([gate[0, columns, :], up[0, columns, :]], axis=1)
        dx = dot(dinner, both, (1, 1)).astype(BF16)
        for unit in range(units):
            for label, part in enumerate(parts):
                here = slice((unit * GROUP + label) * 2 * CAP, (unit * GROUP + label + 1) * 2 * CAP)
                part[pl.ds(unit * 4 * CAP, 2 * CAP), columns] = outs[here]
                part[pl.ds((unit * 4 + 2) * CAP, 2 * CAP), columns] = dx[here]


def grad_kernel(slot_rows, scaled, near_hidden, near_dinner, far_hidden, far_dinner, *refs):
    far, done, near, sems = refs[:3], refs[3], refs[4:7], refs[7]
    done[...] = jnp.zeros_like(done)
    hidden = jnp.concatenate([near_hidden[...], far_hidden[...]], axis=0)
    dinner = jnp.concatenate([near_dinner[...], far_dinner[...]], axis=0)
    middle, hidden_dim = slot_rows.shape[1], hidden.shape[1]
    chunk = chunk_of(middle)
    copies = []
    for index in range(middle // chunk):
        columns = pl.ds(index * chunk, chunk)
        value = dot(slot_rows[:, columns], dinner, (0, 0)).astype(BF16)
        near[0][0, columns, :] = value[:, :hidden_dim]
        near[1][0, columns, :] = value[:, hidden_dim:]
        near[2][0, :, columns] = dot(hidden, scaled[:, columns], (0, 0)).astype(BF16)
        places = [(0, columns), (0, columns), (0, slice(None), columns)]
        for which, at in enumerate(places):
            copies.append(
                pltpu.make_async_copy(near[which].at[at], far[which].at[at], sems.at[which, index])
            )
            copies[-1].start()
    for copy in copies:
        copy.wait()


def merge_kernel(place, scale, *refs):
    outs, nears, sems = refs[-5:-3], refs[-3:-1], refs[-1]
    blocks = refs[:-5]
    middle, parts = blocks[0].shape[1], sems.shape[2]
    chunk = middle // parts
    copies = []
    for side, start in enumerate(halves_of(middle)):
        for part in range(parts):
            here = pl.ds(part * chunk, chunk)
            held = [block[:, here].astype(F32) for block in blocks[side::2]]
            columns = pl.ds(pl.multiple_of(start + part * chunk, 128), chunk)
            for which, (out, near) in enumerate(zip(outs, nears)):
                rows = [value[which * CAP : (which + 1) * CAP] for value in held]
                rows = jnp.concatenate(rows, axis=0)
                if which == 0:
                    rows = rows * scale[:, :1]
                near[:, columns] = dot(place[...], rows.astype(BF16)).astype(BF16)
                sem = sems.at[which, side, part]
                copies.append(pltpu.make_async_copy(near.at[:, columns], out.at[:, columns], sem))
                copies[-1].start()
    for copy in copies:
        copy.wait()


def per_device(tokens, cotangent, expert_ids, gate_weights, w_gate, w_up, w_down):
    flight = lax.axis_size("expert") // GROUP
    tok_count, width = tokens.shape
    middle, hidden_dim = w_gate.shape[1], w_gate.shape[2]
    slots = flight * CAP
    near_rows, far_rows = GROUP * 2 * CAP, (flight - 1) * GROUP * 2 * CAP
    count = near_rows + far_rows
    pair, whole = ((2 * CAP, middle), BF16), ((count, middle), BF16)
    unit, units_shape = ((4 * CAP, middle), BF16), ((4 * CAP * (flight - 1), middle), BF16)
    both = ((2 * CAP * flight, middle), BF16)
    result, token = ((tok_count, width), BF16), ((8, 128), F32)
    weights = [w_gate, w_up, w_down]
    done, open_steps = {}, set()

    def get(name):
        if name not in done:
            if name in open_steps:
                raise ValueError(name)
            open_steps.add(name)
            done[name] = steps[name](name)
        return done[name]

    def run(name, kernel, shapes, operands, **options):
        after = [get(other)[-1] for other in AFTER.get(name, ())]
        return call(kernel, shapes, operands, after=after, cost=COST.get(name, 1), **options)

    def sent(name, block, bit):
        if AFTER.get(name):
            block = run(name, copy_kernel, [(block.shape, BF16)], [block])[0]
        return [neighbour(block, bit)]

    def spread_step(name):
        tree, label = name[0], int(name[1:])
        before, bit = TREES[tree][label]
        return sent(name, get(tree + str(before))[0], bit)

    def reduce_step(name):
        tree, label = name[0], int(name[1:])
        total = summands(tree, label)
        if len(total) > 1:
            total = run(name, add_kernel, [(total[0].shape, BF16)], total)
            return [neighbour(total[0], TREES[tree][label][1])]
        return sent(name, total[0], TREES[tree][label][1])

    def summands(tree, label):
        arrived = [key for key, (before, _) in TREES[tree].items() if before == label]
        return [get(tree)[label]] + [get(tree + str(key))[0] for key in arrived]

    def summed(name, tree, number):
        blocks = summands(tree, 0)
        kernel = functools.partial(split_sum_kernel, len(blocks) - 1)
        return run(name, kernel, [pair] * number, blocks)

    def select(name):
        which = lax.broadcasted_iota(jnp.int32, (2, 1, 1), 0)
        choices = jnp.where(which == 0, expert_ids.T.astype(F32)[None], gate_weights.T[None])
        return run(
            name,
            select_kernel,
            [((tok_count, slots), BF16), ((slots, 128), F32)] + [both] * 2,
            [choices, tokens, cotangent],
            far=(1, 2),
            scratch=[pltpu.VMEM((tok_count, width), BF16)] * 2 + [pltpu.SemaphoreType.DMA((2, 2))],
            limit=52 * 1024 * 1024,
        )

    def far_unit(name):
        units = get("far_there")
        return units if flight == 2 else run(name, stack_kernel, [units_shape], units)

    def far_back(name):
        blocks = summed(name, "C", 2 * (flight - 1))
        parts = []
        for step in range(1, flight):
            parts.append(moved(blocks[2 * step - 2], False, flight - step))
            parts.append(moved(blocks[2 * step - 1], True, flight - step))
        return parts

    def near_back(name):
        own, other = summed(name, "D", 2)
        return [own, moved(other, True, 0)]

    def inner(name):
        pieces = [get(tree + str(label))[0] for tree in "AB" for label in range(GROUP)]
        shapes = [whole, whole, ((count, 3 * hidden_dim), F32)]
        return run(name, inner_kernel, shapes, pieces + weights)

    def returned(name, first, rows, shape):
        partial = get("inner")[2]
        results = run(
            name,
            functools.partial(return_kernel, first),
            [((rows, hidden_dim), BF16), ((rows, 2 * hidden_dim), BF16)] + [shape] * GROUP,
            [partial, get("inner_other")[0]] + weights,
        )
        return results[2:] + results[:2]

    def grads(name):
        shapes = [w_gate.shape, w_up.shape, w_down.shape]
        return run(
            name,
            grad_kernel,
            [(shape, BF16) for shape in shapes] + [token],
            get("inner")[:2] + get("D")[GROUP:] + get("C")[GROUP:],
            far_out=3,
            scratch=[pltpu.VMEM(shape, BF16) for shape in shapes]
            + [pltpu.SemaphoreType.DMA((3, middle // chunk_of(middle)))],
        )

    def merged(name):
        parts = 4 if middle % 512 == 0 else 1
        return run(
            name,
            merge_kernel,
            [result] * 2,
            get("select")[:2] + get("near_back") + get("far_back"),
            far_out=2,
            scratch=[pltpu.VMEM((tok_count, width), BF16)] * 2
            + [pltpu.SemaphoreType.DMA((2, 2, parts))],
        )

    steps = {
        "select": select,
        "near_there": lambda name: [moved(get("select")[3], True, 0)],
        "A0": lambda name: run(
            name, join_kernel, [unit] * flight, [get("select")[2]] + get("near_there")
        ),
        "far_there": lambda name: [
            moved(get("A0")[step], False, step) for step in range(1, flight)
        ],
        "B0": far_unit,
        "inner": inner,
        "inner_other": lambda name: [moved(get("inner")[2], True, 0)],
        "C": lambda name: returned(name, 1, far_rows, units_shape),
        "D": lambda name: returned(name, 0, near_rows, unit),
        "grads": grads,
        "far_back": far_back,
        "near_back": near_back,
        "merged": merged,
    }
    for label in TREES["A"]:
        steps["A" + str(label)] = steps["B" + str(label)] = spread_step
        steps["C" + str(label)] = steps["D" + str(label)] = reduce_step
    for name in ORDER:
        get(name)
    grad_gate, grad_up, grad_down, _ = get("grads")
    mixed_out, input_grad = get("merged")
    return mixed_out, input_grad, grad_gate, grad_up, grad_down


def solution(mesh):
    rows = P(("pipe", "expert"), None)
    columns = P("pipe", None, "expert")
    downs = P("pipe", "expert", None)
    return jax.shard_map(
        per_device,
        mesh=mesh,
        in_specs=(rows, rows, rows, rows, columns, columns, downs),
        out_specs=(rows, rows, columns, columns, downs),
        check_vma=False,
    )
```

```python
import functools

import jax
import jax.numpy as jnp
from jax import lax
from jax.experimental import pallas as pl
from jax.experimental.pallas import tpu as pltpu
from jax.sharding import PartitionSpec as P

GROUP = 8
CAP = 8
BF16, F32 = jnp.bfloat16, jnp.float32
AXES = ("pipe", "expert")
VMEM = pl.BlockSpec(memory_space=pltpu.VMEM)
ANY = pl.BlockSpec(memory_space=pl.ANY)
LIMIT = 16 * 1024 * 1024


TREES = {
    "A": {2: (0, 1), 4: (0, 2), 1: (0, 0), 5: (1, 2), 6: (2, 2), 3: (2, 0), 7: (5, 1)},
    "B": {1: (0, 0), 4: (0, 2), 2: (0, 1), 6: (4, 1), 5: (1, 2), 3: (2, 0), 7: (6, 0)},
    "C": {4: (0, 2), 1: (0, 0), 2: (0, 1), 5: (4, 0), 6: (4, 1), 3: (1, 1), 7: (3, 2)},
    "D": {4: (0, 2), 2: (0, 1), 1: (0, 0), 6: (2, 2), 3: (2, 0), 5: (4, 0), 7: (3, 2)},
}

AFTER = {
    "D4": ["C4"],
    "D1": ["D7", "A1", "D3"],
    "C": ["B3", "inner_other", "B5"],
    "inner": ["B6"],
    "C6": ["inner_other", "inner"],
    "A6": ["A3", "far_there"],
    "A5": ["A4", "A2", "near_there"],
    "D5": ["B7"],
    "A7": ["A2"],
    "D7": ["B4"],
    "C2": ["B7"],
    "merged": ["near_back", "C1"],
    "grads": ["D"],
    "near_back": ["C4"],
    "D2": ["C5"],
    "C4": ["B7"],
    "C1": ["B7"],
    "B1": ["A4"],
}

ORDER = []

COST = {"merged": 20000000, "A0": 4000000, "B0": 1000000, "inner": 20000000, "near_back": 20000000, "grads": 1000000, "select": 20000000, "D": 20000000}


def moved(block, mirror, step):
    ranks, owners = lax.axis_size("pipe"), lax.axis_size("expert")
    route = []
    for rank in range(ranks):
        target = ranks - 1 - rank if mirror else rank
        for index in range(owners):
            route.append((rank * owners + index, target * owners + (index + step * GROUP) % owners))
    return lax.ppermute(block, AXES, route)


def neighbour(block, bit):
    owners = lax.axis_size("expert")
    return lax.ppermute(block, "expert", [(index, index ^ 1 << bit) for index in range(owners)])


def dot(a, b, contract=(1, 0)):
    return lax.dot_general(
        a, b, (((contract[0],), (contract[1],)), ((), ())), preferred_element_type=F32
    )


def call(kernel, shapes, operands, after=(), far=(), far_out=0, scratch=(), cost=1, alias=None, limit=LIMIT):
    out = [jax.ShapeDtypeStruct(shape, dtype) for shape, dtype in shapes]
    count = len(operands)
    specs = [ANY if i in far else VMEM for i in range(count)]

    def body(*refs):
        kernel(*refs[:count], *refs[count + len(after) :])

    results = pl.pallas_call(
        body,
        out_shape=out,
        in_specs=specs + [ANY] * len(after),
        out_specs=[ANY if i < far_out else VMEM for i in range(len(out))],
        scratch_shapes=list(scratch),
        input_output_aliases=alias or {},
        compiler_params=pltpu.CompilerParams(vmem_limit_bytes=limit),
        cost_estimate=pl.CostEstimate(flops=1, bytes_accessed=cost, transcendentals=0),
    )(*operands, *after)
    return list(results)


def copy_kernel(block, out):
    out[...] = block[...]


def add_kernel(*refs):
    total = refs[0][...].astype(F32)
    for ref in refs[1:-1]:
        total = total + ref[...].astype(F32)
    refs[-1][...] = total.astype(BF16)


def join_kernel(own, other, *units):
    for step, out in enumerate(units):
        here = pl.ds(step * 2 * CAP, 2 * CAP)
        mine, theirs = own[here, :].astype(F32), other[here, :].astype(F32)
        unit = jnp.concatenate([mine[:CAP], theirs[:CAP], mine[CAP:], theirs[CAP:]], axis=0)
        out[...] = unit.astype(BF16)


def stack_kernel(*refs):
    rows = refs[0].shape[0]
    for index, ref in enumerate(refs[:-1]):
        refs[-1][pl.ds(index * rows, rows), :] = ref[...]


def split_sum_kernel(arrived, *refs):
    blocks, pieces = refs[: arrived + 1], refs[arrived + 1 :]
    for index in range(0, len(pieces), 2):
        rows = pl.ds(index * 2 * CAP, 4 * CAP)
        unit = blocks[0][rows, :].astype(F32)
        for block in blocks[1:]:
            unit = unit + block[rows, :].astype(F32)
        parts = [unit[place * CAP : (place + 1) * CAP] for place in range(4)]
        pieces[index][...] = jnp.concatenate(parts[0::2], axis=0).astype(BF16)
        pieces[index + 1][...] = jnp.concatenate(parts[1::2], axis=0).astype(BF16)


def halves_of(middle):
    back = lax.axis_index("pipe") >= lax.axis_size("pipe") // 2
    own = pl.multiple_of(back.astype(jnp.int32) * middle, 128)
    return own, pl.multiple_of(middle - own, 128)


def select_kernel(*refs):
    far, near, sems, half_sems = refs[:4], refs[-6:-2], refs[-2], refs[-1]
    ids, gates, tokens, cotangent = near
    place_out, scale_out, *blocks = refs[4:-6]
    middle = blocks[0].shape[1]
    early = [pltpu.make_async_copy(far[i], near[i], sems.at[i]) for i in range(2)]
    halves = []
    for side, start in enumerate(halves_of(middle)):
        columns = pl.ds(start, middle)
        for which in range(2):
            source, target = far[2 + which].at[:, columns], near[2 + which].at[:, columns]
            halves.append(pltpu.make_async_copy(source, target, half_sems.at[side, which]))
    for copy in early + halves:
        copy.start()
    for copy in early:
        copy.wait()
    flight, count = blocks[0].shape[0] // (2 * CAP), ids.shape[1]
    slots = flight * CAP
    column = lax.broadcasted_iota(jnp.int32, (1, slots), 1)
    wanted = lax.axis_index("expert") // GROUP + column // CAP
    wanted = jnp.where(wanted >= flight, wanted - flight, wanted).astype(F32)
    named, weight = ids[...].astype(F32).T, gates[...].T
    hits, chosen = jnp.zeros((count, slots), F32), jnp.zeros((count, slots), F32)
    for choice in range(ids.shape[0]):
        match = (named[:, choice : choice + 1] == wanted).astype(F32)
        hits = hits + match
        chosen = chosen + match * weight[:, choice : choice + 1]
    row = lax.broadcasted_iota(jnp.int32, (count, count), 0)
    earlier = (lax.broadcasted_iota(jnp.int32, (count, count), 1) <= row).astype(BF16)
    slot = dot(earlier, hits.astype(BF16)) - 1.0
    level = (column % CAP).astype(F32)
    place = hits * (slot == level).astype(F32)
    place_bf = place.astype(BF16)
    place_out[...] = place_bf
    scale = lax.dot_general(
        place * chosen,
        jnp.ones((count, 128), F32),
        (((0,), (0,)), ((), ())),
        preferred_element_type=F32,
        precision=lax.Precision.HIGHEST,
    )
    scale_out[...] = scale
    for side, start in enumerate(halves_of(middle)):
        for copy in halves[2 * side : 2 * side + 2]:
            copy.wait()
        rows = dot(place_bf, tokens[:, pl.ds(start, middle)], (0, 0))
        scaled = dot(place_bf, cotangent[:, pl.ds(start, middle)], (0, 0)) * scale[:, :1]
        parts = []
        for step in range(flight):
            here = slice(step * CAP, (step + 1) * CAP)
            parts = parts + [rows[here], scaled[here]]
        blocks[side][...] = jnp.concatenate(parts, axis=0).astype(BF16)


def pair_sum(own, other):
    blocks = [other[pl.ds((index ^ 1) * CAP, CAP), :] for index in range(other.shape[0] // CAP)]
    return own[...] + jnp.concatenate(blocks, axis=0)


def chunk_of(middle):
    return next(size for size in (512, 256, 128) if middle % size == 0)


def inner_kernel(*refs):
    pieces, (gate, up, down, slot_rows, scaled, inner) = refs[:-6], refs[-6:]
    row = 0
    for held in (pieces[:GROUP], pieces[GROUP:]):
        for unit in range(held[0].shape[0] // (4 * CAP)):
            for piece in held:
                here = pl.ds(row, 2 * CAP)
                slot_rows[here, :] = piece[pl.ds(unit * 4 * CAP, 2 * CAP), :]
                scaled[here, :] = piece[pl.ds((unit * 4 + 2) * CAP, 2 * CAP), :]
                row = row + 2 * CAP
    hidden_dim = gate.shape[2]
    both = jnp.concatenate([gate[0], up[0]], axis=1)
    inner[:, : 2 * hidden_dim] = dot(slot_rows[...], both)
    inner[:, 2 * hidden_dim :] = dot(scaled[...], down[0], (1, 1))


def return_kernel(first, own, other, gate, up, down, hidden_out, dinner_out, *parts):
    units = parts[0].shape[0] // (4 * CAP)
    rows = pl.ds(first * GROUP * 2 * CAP, units * GROUP * 2 * CAP)
    inner = pair_sum(own.at[rows, :], other.at[rows, :])
    hidden_dim = gate.shape[2]
    gate_pre, up_pre = inner[:, :hidden_dim], inner[:, hidden_dim : 2 * hidden_dim]
    dhidden = inner[:, 2 * hidden_dim :]
    sigma = jax.nn.sigmoid(gate_pre)
    active = gate_pre * sigma
    hidden = (active * up_pre).astype(BF16)
    dgate = (dhidden * up_pre * sigma * (1.0 + gate_pre * (1.0 - sigma))).astype(BF16)
    dup = (dhidden * active).astype(BF16)
    dinner = jnp.concatenate([dgate, dup], axis=1)
    hidden_out[...] = hidden
    dinner_out[...] = dinner
    middle = gate.shape[1]
    chunk = chunk_of(middle)

    @pl.loop(0, middle // chunk, unroll=True)
    def _(index):
        columns = pl.ds(pl.multiple_of(index * chunk, chunk), chunk)
        outs = dot(hidden, down[0, :, columns]).astype(BF16)
        both = jnp.concatenate([gate[0, columns, :], up[0, columns, :]], axis=1)
        dx = dot(dinner, both, (1, 1)).astype(BF16)
        for unit in range(units):
            for label, part in enumerate(parts):
                here = slice((unit * GROUP + label) * 2 * CAP, (unit * GROUP + label + 1) * 2 * CAP)
                part[pl.ds(unit * 4 * CAP, 2 * CAP), columns] = outs[here]
                part[pl.ds((unit * 4 + 2) * CAP, 2 * CAP), columns] = dx[here]


def grad_kernel(slot_rows, scaled, near_hidden, near_dinner, far_hidden, far_dinner, *refs):
    far, done, near, sems = refs[:3], refs[3], refs[4:7], refs[7]
    done[...] = jnp.zeros_like(done)
    hidden = jnp.concatenate([near_hidden[...], far_hidden[...]], axis=0)
    dinner = jnp.concatenate([near_dinner[...], far_dinner[...]], axis=0)
    middle, hidden_dim = slot_rows.shape[1], hidden.shape[1]
    chunk = chunk_of(middle)
    copies = []
    for index in range(middle // chunk):
        columns = pl.ds(index * chunk, chunk)
        value = dot(slot_rows[:, columns], dinner, (0, 0)).astype(BF16)
        near[0][0, columns, :] = value[:, :hidden_dim]
        near[1][0, columns, :] = value[:, hidden_dim:]
        near[2][0, :, columns] = dot(hidden, scaled[:, columns], (0, 0)).astype(BF16)
        places = [(0, columns), (0, columns), (0, slice(None), columns)]
        for which, at in enumerate(places):
            copies.append(
                pltpu.make_async_copy(near[which].at[at], far[which].at[at], sems.at[which, index])
            )
            copies[-1].start()
    for copy in copies:
        copy.wait()


def merge_kernel(place, scale, *refs):
    outs, nears, sems = refs[-5:-3], refs[-3:-1], refs[-1]
    blocks = refs[:-5]
    middle, parts = blocks[0].shape[1], sems.shape[2]
    chunk = middle // parts
    copies = []
    for side, start in enumerate(halves_of(middle)):
        for part in range(parts):
            here = pl.ds(part * chunk, chunk)
            held = [block[:, here].astype(F32) for block in blocks[side::2]]
            columns = pl.ds(pl.multiple_of(start + part * chunk, 128), chunk)
            for which, (out, near) in enumerate(zip(outs, nears)):
                rows = [value[which * CAP : (which + 1) * CAP] for value in held]
                rows = jnp.concatenate(rows, axis=0)
                if which == 0:
                    rows = rows * scale[:, :1]
                near[:, columns] = dot(place[...], rows.astype(BF16)).astype(BF16)
                sem = sems.at[which, side, part]
                copies.append(pltpu.make_async_copy(near.at[:, columns], out.at[:, columns], sem))
                copies[-1].start()
    for copy in copies:
        copy.wait()


def per_device(tokens, cotangent, expert_ids, gate_weights, w_gate, w_up, w_down):
    flight = lax.axis_size("expert") // GROUP
    tok_count, width = tokens.shape
    middle, hidden_dim = w_gate.shape[1], w_gate.shape[2]
    slots = flight * CAP
    near_rows, far_rows = GROUP * 2 * CAP, (flight - 1) * GROUP * 2 * CAP
    count = near_rows + far_rows
    pair, whole = ((2 * CAP, middle), BF16), ((count, middle), BF16)
    unit, units_shape = ((4 * CAP, middle), BF16), ((4 * CAP * (flight - 1), middle), BF16)
    both = ((2 * CAP * flight, middle), BF16)
    result, token = ((tok_count, width), BF16), ((8, 128), F32)
    weights = [w_gate, w_up, w_down]
    done, open_steps = {}, set()

    def get(name):
        if name not in done:
            if name in open_steps:
                raise ValueError(name)
            open_steps.add(name)
            done[name] = steps[name](name)
        return done[name]

    def run(name, kernel, shapes, operands, **options):
        after = [get(other)[-1] for other in AFTER.get(name, ())]
        return call(kernel, shapes, operands, after=after, cost=COST.get(name, 1), **options)

    def sent(name, block, bit):
        if AFTER.get(name):
            block = run(name, copy_kernel, [(block.shape, BF16)], [block])[0]
        return [neighbour(block, bit)]

    def spread_step(name):
        tree, label = name[0], int(name[1:])
        before, bit = TREES[tree][label]
        return sent(name, get(tree + str(before))[0], bit)

    def reduce_step(name):
        tree, label = name[0], int(name[1:])
        total = summands(tree, label)
        if len(total) > 1:
            total = run(name, add_kernel, [(total[0].shape, BF16)], total)
            return [neighbour(total[0], TREES[tree][label][1])]
        return sent(name, total[0], TREES[tree][label][1])

    def summands(tree, label):
        arrived = [key for key, (before, _) in TREES[tree].items() if before == label]
        return [get(tree)[label]] + [get(tree + str(key))[0] for key in arrived]

    def summed(name, tree, number):
        blocks = summands(tree, 0)
        kernel = functools.partial(split_sum_kernel, len(blocks) - 1)
        return run(name, kernel, [pair] * number, blocks)

    def select(name):
        operands = [expert_ids.T, gate_weights.T, tokens, cotangent]
        return run(
            name,
            select_kernel,
            [((tok_count, slots), BF16), ((slots, 128), F32)] + [both] * 2,
            operands,
            far=range(4),
            scratch=[pltpu.VMEM(x.shape, x.dtype) for x in operands]
            + [pltpu.SemaphoreType.DMA((2,)), pltpu.SemaphoreType.DMA((2, 2))],
            limit=52 * 1024 * 1024,
        )

    def far_unit(name):
        units = get("far_there")
        return units if flight == 2 else run(name, stack_kernel, [units_shape], units)

    def far_back(name):
        blocks = summed(name, "C", 2 * (flight - 1))
        parts = []
        for step in range(1, flight):
            parts.append(moved(blocks[2 * step - 2], False, flight - step))
            parts.append(moved(blocks[2 * step - 1], True, flight - step))
        return parts

    def near_back(name):
        own, other = summed(name, "D", 2)
        return [own, moved(other, True, 0)]

    def inner(name):
        pieces = [get(tree + str(label))[0] for tree in "AB" for label in range(GROUP)]
        shapes = [whole, whole, ((count, 3 * hidden_dim), F32)]
        return run(name, inner_kernel, shapes, pieces + weights)

    def returned(name, first, rows, shape):
        partial = get("inner")[2]
        results = run(
            name,
            functools.partial(return_kernel, first),
            [((rows, hidden_dim), BF16), ((rows, 2 * hidden_dim), BF16)] + [shape] * GROUP,
            [partial, get("inner_other")[0]] + weights,
        )
        return results[2:] + results[:2]

    def grads(name):
        shapes = [w_gate.shape, w_up.shape, w_down.shape]
        return run(
            name,
            grad_kernel,
            [(shape, BF16) for shape in shapes] + [token],
            get("inner")[:2] + get("D")[GROUP:] + get("C")[GROUP:],
            far_out=3,
            scratch=[pltpu.VMEM(shape, BF16) for shape in shapes]
            + [pltpu.SemaphoreType.DMA((3, middle // chunk_of(middle)))],
        )

    def merged(name):
        parts = 4 if middle % 512 == 0 else 1
        return run(
            name,
            merge_kernel,
            [result] * 2,
            get("select")[:2] + get("near_back") + get("far_back"),
            far_out=2,
            scratch=[pltpu.VMEM((tok_count, width), BF16)] * 2
            + [pltpu.SemaphoreType.DMA((2, 2, parts))],
        )

    steps = {
        "select": select,
        "near_there": lambda name: [moved(get("select")[3], True, 0)],
        "A0": lambda name: run(
            name, join_kernel, [unit] * flight, [get("select")[2]] + get("near_there")
        ),
        "far_there": lambda name: [
            moved(get("A0")[step], False, step) for step in range(1, flight)
        ],
        "B0": far_unit,
        "inner": inner,
        "inner_other": lambda name: [moved(get("inner")[2], True, 0)],
        "C": lambda name: returned(name, 1, far_rows, units_shape),
        "D": lambda name: returned(name, 0, near_rows, unit),
        "grads": grads,
        "far_back": far_back,
        "near_back": near_back,
        "merged": merged,
    }
    for label in TREES["A"]:
        steps["A" + str(label)] = steps["B" + str(label)] = spread_step
        steps["C" + str(label)] = steps["D" + str(label)] = reduce_step
    for name in ORDER:
        get(name)
    grad_gate, grad_up, grad_down, _ = get("grads")
    mixed_out, input_grad = get("merged")
    return mixed_out, input_grad, grad_gate, grad_up, grad_down


def solution(mesh):
    rows = P(("pipe", "expert"), None)
    columns = P("pipe", None, "expert")
    downs = P("pipe", "expert", None)
    return jax.shard_map(
        per_device,
        mesh=mesh,
        in_specs=(rows, rows, rows, rows, columns, columns, downs),
        out_specs=(rows, rows, columns, columns, downs),
        check_vma=False,
    )
```

```python
import functools

import jax
import jax.numpy as jnp
from jax import lax
from jax.experimental import pallas as pl
from jax.experimental.pallas import tpu as pltpu
from jax.sharding import PartitionSpec as P

GROUP = 8
CAP = 8
BF16, F32 = jnp.bfloat16, jnp.float32
AXES = ("pipe", "expert")
VMEM = pl.BlockSpec(memory_space=pltpu.VMEM)
ANY = pl.BlockSpec(memory_space=pl.ANY)
LIMIT = 16 * 1024 * 1024


TREES = {
    "A": {4: (0, 2), 1: (0, 0), 2: (0, 1), 5: (1, 2), 6: (2, 2), 3: (2, 0), 7: (5, 1)},
    "B": {1: (0, 0), 4: (0, 2), 2: (0, 1), 6: (4, 1), 5: (1, 2), 3: (2, 0), 7: (6, 0)},
    "C": {4: (0, 2), 1: (0, 0), 2: (0, 1), 5: (4, 0), 6: (4, 1), 3: (1, 1), 7: (3, 2)},
    "D": {4: (0, 2), 2: (0, 1), 1: (0, 0), 6: (2, 2), 3: (2, 0), 5: (4, 0), 7: (3, 2)},
}

AFTER = {
    "D4": ["C4", "C5"],
    "D1": ["D7", "D3"],
    "C": ["B3", "inner_other", "inner", "B7", "B2"],
    "inner": ["B4"],
    "C6": ["inner_other"],
    "A6": ["A3"],
    "A5": ["A4", "near_there"],
    "D5": ["B7"],
    "D7": ["B4"],
    "C2": ["C6"],
    "merged": ["near_back", "C1", "D4", "far_back"],
    "C4": ["C", "C7"],
    "C1": ["C3"],
    "D": ["B7", "inner"],
    "B1": ["A1", "A4"],
    "B2": ["A2"],
    "C7": ["B7"],
    "C3": ["C5"],
    "grads": ["C6"],
    "B7": ["A4"],
    "A4": ["near_there"],
    "D6": ["C6"],
}

ORDER = []

COST = {"merged": 1000000, "A0": 1000000, "C": 4000000, "B0": 1000000, "near_back": 4000000, "D": 4000000, "inner": 4000000, "grads": 20000000, "select": 1000000}


def moved(block, mirror, step):
    ranks, owners = lax.axis_size("pipe"), lax.axis_size("expert")
    route = []
    for rank in range(ranks):
        target = ranks - 1 - rank if mirror else rank
        for index in range(owners):
            route.append((rank * owners + index, target * owners + (index + step * GROUP) % owners))
    return lax.ppermute(block, AXES, route)


def neighbour(block, bit):
    owners = lax.axis_size("expert")
    return lax.ppermute(block, "expert", [(index, index ^ 1 << bit) for index in range(owners)])


def dot(a, b, contract=(1, 0)):
    return lax.dot_general(
        a, b, (((contract[0],), (contract[1],)), ((), ())), preferred_element_type=F32
    )


def call(kernel, shapes, operands, after=(), far=(), far_out=0, scratch=(), cost=1, alias=None, limit=LIMIT):
    out = [jax.ShapeDtypeStruct(shape, dtype) for shape, dtype in shapes]
    count = len(operands)
    specs = [ANY if i in far else VMEM for i in range(count)]

    def body(*refs):
        kernel(*refs[:count], *refs[count + len(after) :])

    results = pl.pallas_call(
        body,
        out_shape=out,
        in_specs=specs + [ANY] * len(after),
        out_specs=[ANY if i < far_out else VMEM for i in range(len(out))],
        scratch_shapes=list(scratch),
        input_output_aliases=alias or {},
        compiler_params=pltpu.CompilerParams(vmem_limit_bytes=limit),
        cost_estimate=pl.CostEstimate(flops=1, bytes_accessed=cost, transcendentals=0),
    )(*operands, *after)
    return list(results)


def copy_kernel(block, out):
    out[...] = block[...]


def add_kernel(*refs):
    total = refs[0][...].astype(F32)
    for ref in refs[1:-1]:
        total = total + ref[...].astype(F32)
    refs[-1][...] = total.astype(BF16)


def join_kernel(own, other, *units):
    for step, out in enumerate(units):
        here = pl.ds(step * 2 * CAP, 2 * CAP)
        mine, theirs = own[here, :].astype(F32), other[here, :].astype(F32)
        unit = jnp.concatenate([mine[:CAP], theirs[:CAP], mine[CAP:], theirs[CAP:]], axis=0)
        out[...] = unit.astype(BF16)


def stack_kernel(*refs):
    rows = refs[0].shape[0]
    for index, ref in enumerate(refs[:-1]):
        refs[-1][pl.ds(index * rows, rows), :] = ref[...]


def split_sum_kernel(arrived, *refs):
    blocks, pieces = refs[: arrived + 1], refs[arrived + 1 :]
    for index in range(0, len(pieces), 2):
        rows = pl.ds(index * 2 * CAP, 4 * CAP)
        unit = blocks[0][rows, :].astype(F32)
        for block in blocks[1:]:
            unit = unit + block[rows, :].astype(F32)
        parts = [unit[place * CAP : (place + 1) * CAP] for place in range(4)]
        pieces[index][...] = jnp.concatenate(parts[0::2], axis=0).astype(BF16)
        pieces[index + 1][...] = jnp.concatenate(parts[1::2], axis=0).astype(BF16)


def halves_of(middle):
    back = lax.axis_index("pipe") >= lax.axis_size("pipe") // 2
    own = pl.multiple_of(back.astype(jnp.int32) * middle, 128)
    return own, pl.multiple_of(middle - own, 128)


def select_kernel(*refs):
    far, near, sems, half_sems = refs[:4], refs[-6:-2], refs[-2], refs[-1]
    ids, gates, tokens, cotangent = near
    place_out, scale_out, *blocks = refs[4:-6]
    middle = blocks[0].shape[1]
    early = [pltpu.make_async_copy(far[i], near[i], sems.at[i]) for i in range(2)]
    halves = []
    for side, start in enumerate(halves_of(middle)):
        columns = pl.ds(start, middle)
        for which in range(2):
            source, target = far[2 + which].at[:, columns], near[2 + which].at[:, columns]
            halves.append(pltpu.make_async_copy(source, target, half_sems.at[side, which]))
    for copy in early + halves:
        copy.start()
    for copy in early:
        copy.wait()
    flight, count = blocks[0].shape[0] // (2 * CAP), ids.shape[1]
    slots = flight * CAP
    column = lax.broadcasted_iota(jnp.int32, (1, slots), 1)
    wanted = lax.axis_index("expert") // GROUP + column // CAP
    wanted = jnp.where(wanted >= flight, wanted - flight, wanted).astype(F32)
    named, weight = ids[...].astype(F32).T, gates[...].T
    hits, chosen = jnp.zeros((count, slots), F32), jnp.zeros((count, slots), F32)
    for choice in range(ids.shape[0]):
        match = (named[:, choice : choice + 1] == wanted).astype(F32)
        hits = hits + match
        chosen = chosen + match * weight[:, choice : choice + 1]
    row = lax.broadcasted_iota(jnp.int32, (count, count), 0)
    earlier = (lax.broadcasted_iota(jnp.int32, (count, count), 1) <= row).astype(BF16)
    slot = dot(earlier, hits.astype(BF16)) - 1.0
    level = (column % CAP).astype(F32)
    place = hits * (slot == level).astype(F32)
    place_bf = place.astype(BF16)
    place_out[...] = place_bf
    scale = lax.dot_general(
        place * chosen,
        jnp.ones((count, 128), F32),
        (((0,), (0,)), ((), ())),
        preferred_element_type=F32,
        precision=lax.Precision.HIGHEST,
    )
    scale_out[...] = scale
    for side, start in enumerate(halves_of(middle)):
        for copy in halves[2 * side : 2 * side + 2]:
            copy.wait()
        rows = dot(place_bf, tokens[:, pl.ds(start, middle)], (0, 0))
        scaled = dot(place_bf, cotangent[:, pl.ds(start, middle)], (0, 0)) * scale[:, :1]
        parts = []
        for step in range(flight):
            here = slice(step * CAP, (step + 1) * CAP)
            parts = parts + [rows[here], scaled[here]]
        blocks[side][...] = jnp.concatenate(parts, axis=0).astype(BF16)


def pair_sum(own, other):
    blocks = [other[pl.ds((index ^ 1) * CAP, CAP), :] for index in range(other.shape[0] // CAP)]
    return own[...] + jnp.concatenate(blocks, axis=0)


def chunk_of(middle):
    return next(size for size in (512, 256, 128) if middle % size == 0)


def inner_kernel(*refs):
    pieces, (gate, up, down, slot_rows, scaled, inner) = refs[:-6], refs[-6:]
    row = 0
    for held in (pieces[:GROUP], pieces[GROUP:]):
        for unit in range(held[0].shape[0] // (4 * CAP)):
            for piece in held:
                here = pl.ds(row, 2 * CAP)
                slot_rows[here, :] = piece[pl.ds(unit * 4 * CAP, 2 * CAP), :]
                scaled[here, :] = piece[pl.ds((unit * 4 + 2) * CAP, 2 * CAP), :]
                row = row + 2 * CAP
    hidden_dim = gate.shape[2]
    both = jnp.concatenate([gate[0], up[0]], axis=1)
    inner[:, : 2 * hidden_dim] = dot(slot_rows[...], both)
    inner[:, 2 * hidden_dim :] = dot(scaled[...], down[0], (1, 1))


def return_kernel(first, own, other, gate, up, down, hidden_out, dinner_out, *parts):
    units = parts[0].shape[0] // (4 * CAP)
    rows = pl.ds(first * GROUP * 2 * CAP, units * GROUP * 2 * CAP)
    inner = pair_sum(own.at[rows, :], other.at[rows, :])
    hidden_dim = gate.shape[2]
    gate_pre, up_pre = inner[:, :hidden_dim], inner[:, hidden_dim : 2 * hidden_dim]
    dhidden = inner[:, 2 * hidden_dim :]
    sigma = jax.nn.sigmoid(gate_pre)
    active = gate_pre * sigma
    hidden = (active * up_pre).astype(BF16)
    dgate = (dhidden * up_pre * sigma * (1.0 + gate_pre * (1.0 - sigma))).astype(BF16)
    dup = (dhidden * active).astype(BF16)
    dinner = jnp.concatenate([dgate, dup], axis=1)
    hidden_out[...] = hidden
    dinner_out[...] = dinner
    middle = gate.shape[1]
    chunk = chunk_of(middle)

    @pl.loop(0, middle // chunk, unroll=True)
    def _(index):
        columns = pl.ds(pl.multiple_of(index * chunk, chunk), chunk)
        outs = dot(hidden, down[0, :, columns]).astype(BF16)
        both = jnp.concatenate([gate[0, columns, :], up[0, columns, :]], axis=1)
        dx = dot(dinner, both, (1, 1)).astype(BF16)
        for unit in range(units):
            for label, part in enumerate(parts):
                here = slice((unit * GROUP + label) * 2 * CAP, (unit * GROUP + label + 1) * 2 * CAP)
                part[pl.ds(unit * 4 * CAP, 2 * CAP), columns] = outs[here]
                part[pl.ds((unit * 4 + 2) * CAP, 2 * CAP), columns] = dx[here]


def grad_kernel(slot_rows, scaled, near_hidden, near_dinner, far_hidden, far_dinner, *refs):
    far, done, near, sems = refs[:3], refs[3], refs[4:7], refs[7]
    done[...] = jnp.zeros_like(done)
    hidden = jnp.concatenate([near_hidden[...], far_hidden[...]], axis=0)
    dinner = jnp.concatenate([near_dinner[...], far_dinner[...]], axis=0)
    middle, hidden_dim = slot_rows.shape[1], hidden.shape[1]
    chunk = chunk_of(middle)
    copies = []
    for index in range(middle // chunk):
        columns = pl.ds(index * chunk, chunk)
        value = dot(slot_rows[:, columns], dinner, (0, 0)).astype(BF16)
        near[0][0, columns, :] = value[:, :hidden_dim]
        near[1][0, columns, :] = value[:, hidden_dim:]
        near[2][0, :, columns] = dot(hidden, scaled[:, columns], (0, 0)).astype(BF16)
        places = [(0, columns), (0, columns), (0, slice(None), columns)]
        for which, at in enumerate(places):
            copies.append(
                pltpu.make_async_copy(near[which].at[at], far[which].at[at], sems.at[which, index])
            )
            copies[-1].start()
    for copy in copies:
        copy.wait()


def merge_kernel(place, scale, *refs):
    outs, nears, sems = refs[-5:-3], refs[-3:-1], refs[-1]
    blocks = refs[:-5]
    middle, parts = blocks[0].shape[1], sems.shape[2]
    chunk = middle // parts
    copies = []
    for side, start in enumerate(halves_of(middle)):
        for part in range(parts):
            here = pl.ds(part * chunk, chunk)
            held = [block[:, here].astype(F32) for block in blocks[side::2]]
            columns = pl.ds(pl.multiple_of(start + part * chunk, 128), chunk)
            for which, (out, near) in enumerate(zip(outs, nears)):
                rows = [value[which * CAP : (which + 1) * CAP] for value in held]
                rows = jnp.concatenate(rows, axis=0)
                if which == 0:
                    rows = rows * scale[:, :1]
                near[:, columns] = dot(place[...], rows.astype(BF16)).astype(BF16)
                sem = sems.at[which, side, part]
                copies.append(pltpu.make_async_copy(near.at[:, columns], out.at[:, columns], sem))
                copies[-1].start()
    for copy in copies:
        copy.wait()


def per_device(tokens, cotangent, expert_ids, gate_weights, w_gate, w_up, w_down):
    flight = lax.axis_size("expert") // GROUP
    tok_count, width = tokens.shape
    middle, hidden_dim = w_gate.shape[1], w_gate.shape[2]
    slots = flight * CAP
    near_rows, far_rows = GROUP * 2 * CAP, (flight - 1) * GROUP * 2 * CAP
    count = near_rows + far_rows
    pair, whole = ((2 * CAP, middle), BF16), ((count, middle), BF16)
    unit, units_shape = ((4 * CAP, middle), BF16), ((4 * CAP * (flight - 1), middle), BF16)
    both = ((2 * CAP * flight, middle), BF16)
    result, token = ((tok_count, width), BF16), ((8, 128), F32)
    weights = [w_gate, w_up, w_down]
    done, open_steps = {}, set()

    def get(name):
        if name not in done:
            if name in open_steps:
                raise ValueError(name)
            open_steps.add(name)
            done[name] = steps[name](name)
        return done[name]

    def run(name, kernel, shapes, operands, **options):
        after = [get(other)[-1] for other in AFTER.get(name, ())]
        return call(kernel, shapes, operands, after=after, cost=COST.get(name, 1), **options)

    def sent(name, block, bit):
        if AFTER.get(name):
            block = run(name, copy_kernel, [(block.shape, BF16)], [block])[0]
        return [neighbour(block, bit)]

    def spread_step(name):
        tree, label = name[0], int(name[1:])
        before, bit = TREES[tree][label]
        return sent(name, get(tree + str(before))[0], bit)

    def reduce_step(name):
        tree, label = name[0], int(name[1:])
        total = summands(tree, label)
        if len(total) > 1:
            total = run(name, add_kernel, [(total[0].shape, BF16)], total)
            return [neighbour(total[0], TREES[tree][label][1])]
        return sent(name, total[0], TREES[tree][label][1])

    def summands(tree, label):
        arrived = [key for key, (before, _) in TREES[tree].items() if before == label]
        return [get(tree)[label]] + [get(tree + str(key))[0] for key in arrived]

    def summed(name, tree, number):
        blocks = summands(tree, 0)
        kernel = functools.partial(split_sum_kernel, len(blocks) - 1)
        return run(name, kernel, [pair] * number, blocks)

    def select(name):
        operands = [expert_ids.T, gate_weights.T, tokens, cotangent]
        return run(
            name,
            select_kernel,
            [((tok_count, slots), BF16), ((slots, 128), F32)] + [both] * 2,
            operands,
            far=range(4),
            scratch=[pltpu.VMEM(x.shape, x.dtype) for x in operands]
            + [pltpu.SemaphoreType.DMA((2,)), pltpu.SemaphoreType.DMA((2, 2))],
            limit=52 * 1024 * 1024,
        )

    def far_unit(name):
        units = get("far_there")
        return units if flight == 2 else run(name, stack_kernel, [units_shape], units)

    def far_back(name):
        blocks = summed(name, "C", 2 * (flight - 1))
        parts = []
        for step in range(1, flight):
            parts.append(moved(blocks[2 * step - 2], False, flight - step))
            parts.append(moved(blocks[2 * step - 1], True, flight - step))
        return parts

    def near_back(name):
        own, other = summed(name, "D", 2)
        return [own, moved(other, True, 0)]

    def inner(name):
        pieces = [get(tree + str(label))[0] for tree in "AB" for label in range(GROUP)]
        shapes = [whole, whole, ((count, 3 * hidden_dim), F32)]
        return run(name, inner_kernel, shapes, pieces + weights)

    def returned(name, first, rows, shape):
        partial = get("inner")[2]
        results = run(
            name,
            functools.partial(return_kernel, first),
            [((rows, hidden_dim), BF16), ((rows, 2 * hidden_dim), BF16)] + [shape] * GROUP,
            [partial, get("inner_other")[0]] + weights,
        )
        return results[2:] + results[:2]

    def grads(name):
        shapes = [w_gate.shape, w_up.shape, w_down.shape]
        return run(
            name,
            grad_kernel,
            [(shape, BF16) for shape in shapes] + [token],
            get("inner")[:2] + get("D")[GROUP:] + get("C")[GROUP:],
            far_out=3,
            scratch=[pltpu.VMEM(shape, BF16) for shape in shapes]
            + [pltpu.SemaphoreType.DMA((3, middle // chunk_of(middle)))],
        )

    def merged(name):
        parts = 4 if middle % 512 == 0 else 1
        return run(
            name,
            merge_kernel,
            [result] * 2,
            get("select")[:2] + get("near_back") + get("far_back"),
            far_out=2,
            scratch=[pltpu.VMEM((tok_count, width), BF16)] * 2
            + [pltpu.SemaphoreType.DMA((2, 2, parts))],
        )

    steps = {
        "select": select,
        "near_there": lambda name: [moved(get("select")[3], True, 0)],
        "A0": lambda name: run(
            name, join_kernel, [unit] * flight, [get("select")[2]] + get("near_there")
        ),
        "far_there": lambda name: [
            moved(get("A0")[step], False, step) for step in range(1, flight)
        ],
        "B0": far_unit,
        "inner": inner,
        "inner_other": lambda name: [moved(get("inner")[2], True, 0)],
        "C": lambda name: returned(name, 1, far_rows, units_shape),
        "D": lambda name: returned(name, 0, near_rows, unit),
        "grads": grads,
        "far_back": far_back,
        "near_back": near_back,
        "merged": merged,
    }
    for label in TREES["A"]:
        steps["A" + str(label)] = steps["B" + str(label)] = spread_step
        steps["C" + str(label)] = steps["D" + str(label)] = reduce_step
    for name in ORDER:
        get(name)
    grad_gate, grad_up, grad_down, _ = get("grads")
    mixed_out, input_grad = get("merged")
    return mixed_out, input_grad, grad_gate, grad_up, grad_down


def solution(mesh):
    rows = P(("pipe", "expert"), None)
    columns = P("pipe", None, "expert")
    downs = P("pipe", "expert", None)
    return jax.shard_map(
        per_device,
        mesh=mesh,
        in_specs=(rows, rows, rows, rows, columns, columns, downs),
        out_specs=(rows, rows, columns, columns, downs),
        check_vma=False,
    )
```
